256 devices in a mesh: gx: 8 (over y, x_hi), gy: 8 (over z), gz: 4 (over x_lo, core).
Axes of the slice: x: 4 (x_hi: 2, x_lo: 2; x = x_hi * 2 + x_lo), y: 4, z: 8, core: 2. Of those that a mesh axis runs over, the one named last changes fastest.
Arguments:
- populations: float32 [19, 128, 128, 512], P(None, 'gx', 'gy', 'gz'), may hold values from 0.02 to 0.1
- solid_flags: int32 [128, 128, 512], P('gx', 'gy', 'gz'), may hold values 0 or 1
- positions: float32 [7168, 3, 128], P(('gx', 'gy', 'gz')), may hold values from -4 to 4
- anchors: float32 [7168, 3, 128], P(('gx', 'gy', 'gz')), may hold values from -4 to 4
- base_cell: int32 [7168, 3, 128], P(('gx', 'gy', 'gz')), may hold values from 0 to 510, as said below
- weights: float32 [7168, 8, 128], P(('gx', 'gy', 'gz')), may hold values from 0.1 to 0.2
- intersection: int32 [7168, 2], P(('gx', 'gy', 'gz')), may hold values from 0 to 31, as said below
Outputs:
- read: float32 [19, 128, 128, 512], P(None, 'gx', 'gy', 'gz')
- vertex_velocity: float32 [7168, 3, 128], P(('gx', 'gy', 'gz'))
The draws below stay inside these ranges and needn't reach their ends.
Inputs may be any that keep to these rules, and one draw needn't show every extreme that they name: `intersection`: patch p's two bricks differ and lie in its owner's slab. For every owner, no brick is listed by more than 4 of its patches, and in every slab a quarter of the bricks are listed by exactly 4 patches of every owner of that slab. `base_cell`: all eight kernel cells of a vertex lie in one brick, in the slab of the patch's owner, and that brick is on the patch's list.
All inputs are finite; a program needn't handle non-finite values. No bound on the sum of `solid_flags` on one device may be relied on, other than what follows from the above.
Results may differ from the reference program's by a relative error of at most 0.00011.
Values sent between devices are 32-bit elements; how exact they have to be, the bound alone decides.
A program may use at most 320 MiB of HBM per device.

```python
import jax
import jax.numpy as jnp
import numpy as np
from jax import lax

CX = 16
CY = 16
CZ = 128
VERT = 128
SLOT_CAP = 4
SLABS = 8
BRICKS_Z = 4
BRICKS = 32
PATCH_DEV = 28
PATCHES = 7168
NX = 128
NY = 128
NZ = 512


def intersection_table(key):
    counts = np.where(np.arange(BRICKS) < BRICKS // 4, SLOT_CAP, SLOT_CAP // 4)
    rank_list = np.repeat(np.arange(BRICKS), counts)
    slab_keys = jax.random.split(jax.random.fold_in(key, 101), SLABS)
    dense_rank = jax.vmap(lambda sub_key: jax.random.permutation(sub_key, BRICKS))(slab_keys)
    grouped = dense_rank[:, rank_list].astype(jnp.int32)
    owner_keys = jax.random.split(jax.random.fold_in(key, 202), SLABS * BRICKS)
    patch_order = jax.vmap(lambda sub_key: jax.random.permutation(sub_key, PATCH_DEV))(owner_keys)
    patch_order = patch_order.reshape(SLABS, BRICKS, PATCH_DEV).astype(jnp.int32)
    spread_out = jnp.broadcast_to(grouped[:, None, :], (SLABS, BRICKS, 2 * PATCH_DEV))
    first_brick = jnp.take_along_axis(spread_out, patch_order, 2)
    second_brick = jnp.take_along_axis(spread_out, patch_order + PATCH_DEV, 2)
    swapped = jax.random.randint(jax.random.fold_in(key, 303), (SLABS, BRICKS, PATCH_DEV), 0, 2)
    left_brick = jnp.where(swapped == 1, second_brick, first_brick)
    right_brick = jnp.where(swapped == 1, first_brick, second_brick)
    return jnp.stack([left_brick, right_brick], axis=-1).reshape(PATCHES, 2).astype(jnp.int32)


def draw_intersection(key, part):
    return intersection_table(key)


def draw_base_cell(key, part):
    lists = intersection_table(key)
    which_brick = jax.random.randint(jax.random.fold_in(key, 404), (PATCHES, VERT), 0, 2)
    home_brick = jnp.where(which_brick == 0, lists[:, 0:1], lists[:, 1:2])
    owner_slab = (jnp.arange(PATCHES, dtype=jnp.int32) // (PATCH_DEV * BRICKS))[:, None]
    cell_x = owner_slab * CX + jax.random.randint(jax.random.fold_in(key, 505), (PATCHES, VERT), 0, CX - 1)
    cell_y = home_brick // BRICKS_Z * CY + jax.random.randint(jax.random.fold_in(key, 606), (PATCHES, VERT), 0, CY - 1)
    cell_z = home_brick % BRICKS_Z * CZ + jax.random.randint(jax.random.fold_in(key, 707), (PATCHES, VERT), 0, CZ - 1)
    return jnp.stack([cell_x, cell_y, cell_z], axis=1).astype(jnp.int32)


def touch_ends(values, rng, low, high):
    longest = values.shape.index(max(values.shape))
    spots = []
    for shift in (0, 1):
        where = [jax.random.randint(jax.random.fold_in(rng, axis), (), 0, length) for axis, length in enumerate(values.shape)]
        where[longest] = (where[longest] + shift) % values.shape[longest]
        spots.append(tuple(where))
    return values.at[spots[0]].set(low).at[spots[1]].set(high)


def block_scale(stream_key, extent, cuts, least, top_value):
    loudness, own = 1.0, jax.random.fold_in(stream_key, 6)
    for position, shards_of in cuts:
        heights = jnp.exp(jax.random.uniform(jax.random.fold_in(own, position), (shards_of,), jnp.float32, least / len(cuts), top_value / len(cuts)))
        loudness = loudness * jnp.repeat(heights, extent[position] // shards_of).reshape([-1 if axis == position else 1 for axis in range(len(extent))])
    return loudness


def bell_draw(key, dims, spread, bound, cuts=(), held_as=jnp.bfloat16):
    level = block_scale(key, dims, cuts, -0.22, 0.18) if cuts else 1.0
    drawn = jax.random.normal(key, dims, jnp.float32) * spread * level
    return jnp.minimum(jnp.maximum(drawn, -bound), bound).astype(held_as)


def setup_inputs(seed: int = 0) -> dict:
    keys = jax.random.split(jax.random.key(seed), 8)
    populations = jnp.clip(0.02 + 0.08 * jax.random.uniform(keys[0], (19, NX, NY, NZ), jnp.float32) ** block_scale(keys[0], (19, NX, NY, NZ), ((1, 8), (2, 8), (3, 4)), -0.2, 0.2), 0.02, 0.1)
    solid_flags = touch_ends((jax.random.randint(keys[1], (NX, NY, NZ), 0, 8) < 1).astype(jnp.int32), jax.random.fold_in(keys[1], 1), 0, 1)
    positions = bell_draw(keys[2], (PATCHES, 3, VERT), 1.0, 4.0, ((0, 256),), jnp.float32)
    anchors = bell_draw(keys[3], (PATCHES, 3, VERT), 1.0, 4.0, ((0, 256),), jnp.float32)
    base_cell = draw_base_cell(jax.random.fold_in(keys[7], 71), 0)
    weights = jnp.clip(0.1 + 0.1 * jax.random.uniform(keys[5], (PATCHES, 8, VERT), jnp.float32) ** block_scale(keys[5], (PATCHES, 8, VERT), ((0, 256),), -0.2, 0.2), 0.1, 0.2)
    intersection = draw_intersection(jax.random.fold_in(keys[7], 71), 0)
    return dict(populations=populations, solid_flags=solid_flags, positions=positions, anchors=anchors, base_cell=base_cell, weights=weights, intersection=intersection)


RELAXATION = 0.8
TENSION = 0.05
TETHER = 0.5
VELOCITIES = [(0, 0, 0), (1, 0, 0), (-1, 0, 0), (0, 1, 0), (0, -1, 0), (0, 0, 1), (0, 0, -1),
              (1, 1, 0), (-1, -1, 0), (1, -1, 0), (-1, 1, 0), (1, 0, 1), (-1, 0, -1),
              (1, 0, -1), (-1, 0, 1), (0, 1, 1), (0, -1, -1), (0, 1, -1), (0, -1, 1)]
OPPOSITE = [0, 2, 1, 4, 3, 6, 5, 8, 7, 10, 9, 12, 11, 14, 13, 16, 15, 18, 17]
LATTICE_WEIGHTS = [1.0 / 3.0] + [1.0 / 18.0] * 6 + [1.0 / 36.0] * 12


def membrane_force(positions, anchors):
    cycle_term = jnp.roll(positions, 1, axis=2) + jnp.roll(positions, -1, axis=2) - 2.0 * positions
    return TENSION * cycle_term + TETHER * (anchors - positions)


def collide(populations, solid_flags, force_field):
    lattice = jnp.asarray(VELOCITIES, jnp.float32)
    density = jnp.sum(populations, axis=0)
    momentum = jnp.einsum("qa,qxyz->axyz", lattice, populations, precision=lax.Precision.HIGHEST)
    velocity = (momentum + 0.5 * force_field) / density
    speed_sq = velocity[0] * velocity[0] + velocity[1] * velocity[1] + velocity[2] * velocity[2]
    u_dot_f = velocity[0] * force_field[0] + velocity[1] * force_field[1] + velocity[2] * force_field[2]
    factor = 1.0 - 0.5 / RELAXATION
    outputs = []
    for direction in range(19):
        move_x, move_y, move_z = VELOCITIES[direction]
        along_u = move_x * velocity[0] + move_y * velocity[1] + move_z * velocity[2]
        along_f = move_x * force_field[0] + move_y * force_field[1] + move_z * force_field[2]
        weight_q = LATTICE_WEIGHTS[direction]
        equilibrium = weight_q * density * (1.0 + 3.0 * along_u + 4.5 * along_u * along_u - 1.5 * speed_sq)
        forcing = factor * weight_q * (3.0 * (along_f - u_dot_f) + 9.0 * along_u * along_f)
        current = populations[direction]
        relaxed = current - (current - equilibrium) / RELAXATION + forcing
        outputs.append(jnp.where(solid_flags == 1, populations[OPPOSITE[direction]], relaxed))
    return jnp.stack(outputs), velocity


def reference(populations, solid_flags, positions, anchors, base_cell, weights, intersection):
    forces = membrane_force(positions, anchors)
    owner_slab = jnp.arange(PATCHES, dtype=jnp.int32) // (PATCH_DEV * BRICKS)
    cell_x = base_cell[:, 0, :]
    cell_y = base_cell[:, 1, :]
    cell_z = base_cell[:, 2, :]
    home_brick = (cell_y // CY) * BRICKS_Z + cell_z // CZ
    live_mask = (cell_x // CX == owner_slab[:, None]) & ((home_brick == intersection[:, 0:1]) | (home_brick == intersection[:, 1:2]))
    kernel = weights * live_mask[:, None, :].astype(jnp.float32)
    force_field = jnp.zeros((3, NX * NY * NZ), jnp.float32)
    index_list = []
    for corner in range(8):
        offset_x = (corner >> 2) & 1
        offset_y = (corner >> 1) & 1
        offset_z = corner & 1
        cell_index = ((cell_x + offset_x) * NY + cell_y + offset_y) * NZ + cell_z + offset_z
        cell_index = cell_index.astype(jnp.int32).reshape(-1)
        index_list.append(cell_index)
        contrib = kernel[:, corner, :][:, None, :] * forces
        force_field = force_field.at[:, cell_index].add(jnp.transpose(contrib, (1, 0, 2)).reshape(3, -1))
    force_field = force_field.reshape(3, NX, NY, NZ)
    post_collision, velocity = collide(populations, solid_flags, force_field)
    read = jnp.stack([jnp.roll(post_collision[direction], VELOCITIES[direction], (0, 1, 2)) for direction in range(19)])
    flat_velocity = velocity.reshape(3, -1)
    vertex_velocity = jnp.zeros((PATCHES, 3, VERT), jnp.float32)
    for corner in range(8):
        sampled = jnp.transpose(flat_velocity[:, index_list[corner]].reshape(3, PATCHES, VERT), (1, 0, 2))
        vertex_velocity = vertex_velocity + kernel[:, corner, :][:, None, :] * sampled
    return read, vertex_velocity
```

```python
import jax
import jax.numpy as jnp
from jax import lax
from jax.experimental import pallas as pl
from jax.experimental.pallas import tpu as pltpu
from jax.sharding import PartitionSpec as P

SLOT_CAP = 4
VERT = 128
BRICKS = 32
PATCH_DEV = 28
ROWS = 56
HALF = 9 * 16

RELAXATION = 0.8
TENSION = 0.05
TETHER = 0.5
VELOCITIES = [
    (0, 0, 0),
    (1, 0, 0),
    (-1, 0, 0),
    (0, 1, 0),
    (0, -1, 0),
    (0, 0, 1),
    (0, 0, -1),
    (1, 1, 0),
    (-1, -1, 0),
    (1, -1, 0),
    (-1, 1, 0),
    (1, 0, 1),
    (-1, 0, -1),
    (1, 0, -1),
    (-1, 0, 1),
    (0, 1, 1),
    (0, -1, -1),
    (0, 1, -1),
    (0, -1, 1),
]
OPPOSITE = [0, 2, 1, 4, 3, 6, 5, 8, 7, 10, 9, 12, 11, 14, 13, 16, 15, 18, 17]
LATTICE_WEIGHTS = [1.0 / 3.0] + [1.0 / 18.0] * 6 + [1.0 / 36.0] * 12
F32 = jnp.float32
BF16 = jnp.bfloat16
OUTSIDE = -100.0


def prep_kernel(inter_ref, pos_ref, anc_ref, cell_ref, w_ref, out_ref, tgt_ref, count_ref):
    root_x = lax.axis_index("gx") * 16

    def clear_count(b, carry):
        count_ref[b] = 0
        return carry

    lax.fori_loop(0, BRICKS, clear_count, 0)

    def clear(b, carry):
        out_ref[b, 0:44] = jnp.zeros((44, VERT), F32)
        out_ref[b, 44:56] = jnp.full((12, VERT), OUTSIDE, F32)
        return carry

    lax.fori_loop(0, BRICKS, clear, 0)

    def patch(p, carry):
        pos = pos_ref[p]
        cycle = pltpu.roll(pos, 1, 1) + pltpu.roll(pos, VERT - 1, 1) - 2.0 * pos
        force = TENSION * cycle + TETHER * (anc_ref[p] - pos)
        cell = cell_ref[p]
        weight = w_ref[p]
        for j in range(2):
            b = inter_ref[p, j]
            r = count_ref[b]
            count_ref[b] = r + 1
            tgt_ref[p, j] = b * SLOT_CAP + r
            x = cell[0:1] - root_x
            y = cell[1:2] - (b // 4) * 16
            z = cell[2:3] - (b % 4) * 128
            inside = (x >= 0) & (x < 16) & (y >= 0) & (y < 16) & (z >= 0) & (z < 128)
            out_ref[b, pl.ds(pl.multiple_of(r * 8, 8), 8)] = weight
            for a, coord in enumerate((x, y, z)):
                out_ref[b, pl.ds(32 + 4 * a + r, 1)] = force[a : a + 1]
                out_ref[b, pl.ds(44 + 4 * a + r, 1)] = jnp.where(
                    inside, coord.astype(F32), OUTSIDE
                )
        return carry

    lax.fori_loop(0, PATCH_DEV, patch, 0)


def prep(intersection, positions, anchors, base_cell, weights):
    vmem = pl.BlockSpec(memory_space=pltpu.VMEM)
    smem = pl.BlockSpec(memory_space=pltpu.SMEM)
    return pl.pallas_call(
        prep_kernel,
        name="prep",
        out_shape=(
            jax.ShapeDtypeStruct((BRICKS, ROWS, VERT), F32),
            jax.ShapeDtypeStruct((PATCH_DEV, 2), jnp.int32),
        ),
        in_specs=[smem, vmem, vmem, vmem, vmem],
        out_specs=(vmem, smem),
        scratch_shapes=[pltpu.SMEM((BRICKS,), jnp.int32)],
    )(intersection, positions, anchors, base_cell, weights)


def halves(value):
    high = value.astype(BF16)
    return high, (value - high.astype(F32)).astype(BF16)


def scatter_chunk(tab_ref, i, a_ref, z_ref, acc_ref):
    y_iota = lax.broadcasted_iota(jnp.int32, (16, VERT), 0).astype(F32)
    z_iota = lax.broadcasted_iota(jnp.int32, (256, VERT), 0).astype(F32)
    zero16 = jnp.zeros((16, VERT), BF16)
    for s in range(SLOT_CAP):
        x = tab_ref[i, pl.ds(44 + s, 1)]
        y = tab_ref[i, pl.ds(48 + s, 1)]
        z = tab_ref[i, pl.ds(52 + s, 1)]
        upper = x >= 8.0
        x_in = jnp.where(upper, x - 8.0, x)
        column = jnp.where(upper, z + 128.0, z)
        lanes = slice(s * VERT, (s + 1) * VERT)
        z_ref[:, lanes] = jnp.where(z_iota == column, 1.0, 0.0).astype(BF16)
        at_y = y_iota == y
        at_y1 = y_iota - 1.0 == y
        x_wide = jnp.broadcast_to(x_in, (16, VERT)).astype(BF16)
        masks = [x_wide == jnp.asarray(k, BF16) for k in range(-1, 9)]
        for kz in range(2):
            for c in range(3):
                force = tab_ref[i, pl.ds(32 + 4 * c + s, 1)]
                parts = []
                for kx in range(2):
                    w0 = tab_ref[i, pl.ds(8 * s + 4 * kx + kz, 1)] * force
                    w1 = tab_ref[i, pl.ds(8 * s + 4 * kx + 2 + kz, 1)] * force
                    parts.append(halves(jnp.where(at_y, w0, jnp.where(at_y1, w1, 0.0))))
                base = (kz * 3 + c) * HALF
                for hl in range(2):
                    col = slice(hl * 512 + s * VERT, hl * 512 + (s + 1) * VERT)
                    for plane in range(9):
                        a_ref[base + plane * 16 : base + plane * 16 + 16, col] = jnp.where(
                            masks[plane + 1],
                            parts[0][hl],
                            jnp.where(masks[plane], parts[1][hl], zero16),
                        )
    zz = z_ref[...]
    for block in range(6):
        rows = slice(block * HALF, (block + 1) * HALF)
        dims = (((1,), (1,)), ((), ()))
        acc_ref[rows] += lax.dot_general(
            a_ref[rows, 0:512], zz, dims, preferred_element_type=F32
        ) + lax.dot_general(a_ref[rows, 512:1024], zz, dims, preferred_element_type=F32)


def finish_force(acc_ref, force_ref):
    for c in range(3):
        for plane in range(16):
            pair = []
            for kz in range(2):
                base = (kz * 3 + c) * HALF
                if plane < 8:
                    total = acc_ref[base + plane * 16 : base + plane * 16 + 16, 0:128]
                elif plane == 8:
                    total = (
                        acc_ref[base + 128 : base + 144, 0:128]
                        + acc_ref[base : base + 16, 128:256]
                    )
                else:
                    start = base + (plane - 8) * 16
                    total = acc_ref[start : start + 16, 128:256]
                pair.append(total)
            force_ref[c, plane * 16 : plane * 16 + 16] = pair[0] + pltpu.roll(pair[1], 1, 1)


def collide_all(pop_ref, solid_ref, force_ref, post_ref, vel_ref):
    factor = 1.0 - 0.5 / RELAXATION

    def chunk(step, carry):
        x = step // 2
        yy = pl.ds(pl.multiple_of((step % 2) * 8, 8), 8)
        rows = pl.ds(pl.multiple_of(step * 8, 8), 8)
        pops = [pop_ref[q, x, yy] for q in range(19)]
        solid = solid_ref[x, yy] == 1
        force = [force_ref[c, rows] for c in range(3)]
        density = sum(pops[1:], pops[0])
        inverse = 1.0 / density
        velocity = []
        for a in range(3):
            plus = [pops[q] for q in range(19) if VELOCITIES[q][a] == 1]
            minus = [pops[q] for q in range(19) if VELOCITIES[q][a] == -1]
            momentum = sum(plus[1:], plus[0]) - sum(minus[1:], minus[0])
            u = (momentum + 0.5 * force[a]) * inverse
            velocity.append(u)
            vel_ref[a, rows] = u
        speed_sq = velocity[0] * velocity[0] + velocity[1] * velocity[1] + velocity[2] * velocity[2]
        u_dot_f = velocity[0] * force[0] + velocity[1] * force[1] + velocity[2] * force[2]
        common = 1.0 - 1.5 * speed_sq

        def along(direction, parts):
            total = None
            for step_a, part in zip(direction, parts):
                if step_a:
                    term = part if step_a == 1 else -part
                    total = term if total is None else total + term
            return total

        for q in range(19):
            w = LATTICE_WEIGHTS[q]
            if q == 0:
                equilibrium = w * density * common
                forcing = (factor * w) * (-3.0 * u_dot_f)
            else:
                along_u = along(VELOCITIES[q], velocity)
                along_f = along(VELOCITIES[q], force)
                equilibrium = w * density * (common + along_u * (3.0 + 4.5 * along_u))
                forcing = (factor * w) * (3.0 * (along_f - u_dot_f) + 9.0 * along_u * along_f)
            relaxed = pops[q] - (pops[q] - equilibrium) * (1.0 / RELAXATION) + forcing
            post_ref[q, x, yy] = jnp.where(solid, pops[OPPOSITE[q]], relaxed)
        return carry

    lax.fori_loop(0, 32, chunk, 0)


def transpose_velocity(vel_ref, vt_ref):
    for c in range(3):
        high, low = halves(vel_ref[c].T)
        rows = slice(c * 128, (c + 1) * 128)
        vt_ref[rows, 0:256] = high
        vt_ref[rows, 256:512] = high
        vt_ref[rows, 512:768] = low


def gather_chunk(tab_ref, i, b_ref, vt_ref, ret_ref):
    y_iota = lax.broadcasted_iota(jnp.int32, (16, VERT), 0).astype(F32)
    z_iota = lax.broadcasted_iota(jnp.int32, (VERT, VERT), 0).astype(F32)
    zero16 = jnp.zeros((16, VERT), BF16)
    for s in range(SLOT_CAP):
        x = tab_ref[i, pl.ds(44 + s, 1)]
        y = tab_ref[i, pl.ds(48 + s, 1)]
        z = tab_ref[i, pl.ds(52 + s, 1)]
        at_y = y_iota == y
        at_y1 = y_iota - 1.0 == y
        x_wide = jnp.broadcast_to(x, (16, VERT)).astype(BF16)
        masks = [x_wide == jnp.asarray(k, BF16) for k in range(-1, 16)]
        for kz in range(2):
            parts = []
            for kx in range(2):
                w0 = tab_ref[i, pl.ds(8 * s + 4 * kx + kz, 1)]
                w1 = tab_ref[i, pl.ds(8 * s + 4 * kx + 2 + kz, 1)]
                parts.append(halves(jnp.where(at_y, w0, jnp.where(at_y1, w1, 0.0))))
            cols = slice(kz * VERT, (kz + 1) * VERT)
            for hl in range(2):
                for plane in range(16):
                    value = jnp.where(
                        masks[plane + 1],
                        parts[0][hl],
                        jnp.where(masks[plane], parts[1][hl], zero16),
                    )
                    row = hl * 256 + plane * 16
                    b_ref[s, row : row + 16, cols] = value
                    if hl == 0:
                        b_ref[s, 512 + plane * 16 : 528 + plane * 16, cols] = value
        picked = jnp.dot(vt_ref[...], b_ref[s], preferred_element_type=F32)
        at_z = z_iota == z
        at_z1 = z_iota - 1.0 == z
        for c in range(3):
            rows = slice(c * 128, (c + 1) * 128)
            both = jnp.where(at_z, picked[rows, 0:128], 0.0) + jnp.where(
                at_z1, picked[rows, 128:256], 0.0
            )
            ret_ref[i, pl.ds(4 * c + s, 1)] = jnp.sum(both, axis=0, keepdims=True)


def core_kernel(
    tab_ref, pop_ref, solid_ref, post_ref, ret_ref, a_ref, z_ref, acc_ref, force_ref, vel_ref, vt_ref, b_ref
):
    acc_ref[...] = jnp.zeros_like(acc_ref)

    def scatter(i, carry):
        scatter_chunk(tab_ref, i, a_ref, z_ref, acc_ref)
        return carry

    lax.fori_loop(0, BRICKS, scatter, 0)
    finish_force(acc_ref, force_ref)
    collide_all(pop_ref, solid_ref, force_ref, post_ref, vel_ref)
    transpose_velocity(vel_ref, vt_ref)

    def gather(i, carry):
        gather_chunk(tab_ref, i, b_ref, vt_ref, ret_ref)
        return carry

    lax.fori_loop(0, BRICKS, gather, 0)


def core(table, populations, solid_flags):
    vmem = pl.BlockSpec(memory_space=pltpu.VMEM)
    return pl.pallas_call(
        core_kernel,
        name="core",
        out_shape=(
            jax.ShapeDtypeStruct(populations.shape, F32),
            jax.ShapeDtypeStruct((BRICKS, 12, VERT), F32),
        ),
        in_specs=[vmem] * 3,
        out_specs=(vmem, vmem),
        scratch_shapes=[
            pltpu.VMEM((6 * HALF, 1024), BF16),
            pltpu.VMEM((256, 512), BF16),
            pltpu.VMEM((6 * HALF, 256), F32),
            pltpu.VMEM((3, 256, 128), F32),
            pltpu.VMEM((3, 256, 128), F32),
            pltpu.VMEM((384, 768), BF16),
            pltpu.VMEM((4, 768, 256), BF16),
        ],
        compiler_params=pltpu.CompilerParams(vmem_limit_bytes=32 * 1024 * 1024),
    )(table, populations, solid_flags)


def combine_kernel(tgt_ref, returned_ref, out_ref):
    def patch(p, carry):
        first, second = tgt_ref[p, 0], tgt_ref[p, 1]
        for c in range(3):
            out_ref[p, c : c + 1] = (
                returned_ref[first // SLOT_CAP, pl.ds(4 * c + first % SLOT_CAP, 1)]
                + returned_ref[second // SLOT_CAP, pl.ds(4 * c + second % SLOT_CAP, 1)]
            )
        return carry

    lax.fori_loop(0, PATCH_DEV, patch, 0)


def combine(target, returned):
    vmem = pl.BlockSpec(memory_space=pltpu.VMEM)
    return pl.pallas_call(
        combine_kernel,
        name="combine",
        out_shape=jax.ShapeDtypeStruct((PATCH_DEV, 3, VERT), F32),
        in_specs=[pl.BlockSpec(memory_space=pltpu.SMEM), vmem],
        out_specs=vmem,
    )(target, returned)


def stream(post):
    lists = [post[q] for q in range(19)]
    for dim, axis in enumerate(("gx", "gy", "gz")):
        plus = [q for q in range(19) if VELOCITIES[q][dim] == 1]
        minus = [q for q in range(19) if VELOCITIES[q][dim] == -1]
        size = lists[0].shape[dim]
        count = lax.axis_size(axis)
        up = jnp.stack([lax.slice_in_dim(lists[q], size - 1, size, axis=dim) for q in plus])
        down = jnp.stack([lax.slice_in_dim(lists[q], 0, 1, axis=dim) for q in minus])
        before = lax.ppermute(up, axis, [(i, (i + 1) % count) for i in range(count)])
        after = lax.ppermute(down, axis, [((i + 1) % count, i) for i in range(count)])
        for k, q in enumerate(plus):
            body = lax.slice_in_dim(lists[q], 0, size - 1, axis=dim)
            lists[q] = jnp.concatenate([before[k], body], axis=dim)
        for k, q in enumerate(minus):
            body = lax.slice_in_dim(lists[q], 1, size, axis=dim)
            lists[q] = jnp.concatenate([body, after[k]], axis=dim)
    return jnp.stack(lists)


def body(populations, solid_flags, positions, anchors, base_cell, weights, intersection):
    outgoing, target = prep(intersection, positions, anchors, base_cell, weights)
    table = lax.all_to_all(outgoing, ("gy", "gz"), split_axis=0, concat_axis=0, tiled=True)
    post, summed = core(table, populations, solid_flags)
    returned = lax.all_to_all(summed, ("gy", "gz"), split_axis=0, concat_axis=0, tiled=True)
    vertex_velocity = combine(target, returned)
    return (stream(post), vertex_velocity)


def solution(mesh):
    return jax.shard_map(
        body,
        mesh=mesh,
        in_specs=(
            P(None, "gx", "gy", "gz"),
            P("gx", "gy", "gz"),
            P(("gx", "gy", "gz"), None, None),
            P(("gx", "gy", "gz"), None, None),
            P(("gx", "gy", "gz"), None, None),
            P(("gx", "gy", "gz"), None, None),
            P(("gx", "gy", "gz"), None),
        ),
        out_specs=(P(None, "gx", "gy", "gz"), P(("gx", "gy", "gz"), None, None)),
        check_vma=False,
    )
```

```python
import jax
import jax.numpy as jnp
from jax import lax
from jax.experimental import pallas as pl
from jax.experimental.pallas import tpu as pltpu
from jax.sharding import PartitionSpec as P

SLOT_CAP = 4
VERT = 128
BRICKS = 32
PATCH_DEV = 28
ROWS = 56
HALF = 9 * 16

RELAXATION = 0.8
TENSION = 0.05
TETHER = 0.5
VELOCITIES = [
    (0, 0, 0),
    (1, 0, 0),
    (-1, 0, 0),
    (0, 1, 0),
    (0, -1, 0),
    (0, 0, 1),
    (0, 0, -1),
    (1, 1, 0),
    (-1, -1, 0),
    (1, -1, 0),
    (-1, 1, 0),
    (1, 0, 1),
    (-1, 0, -1),
    (1, 0, -1),
    (-1, 0, 1),
    (0, 1, 1),
    (0, -1, -1),
    (0, 1, -1),
    (0, -1, 1),
]
OPPOSITE = [0, 2, 1, 4, 3, 6, 5, 8, 7, 10, 9, 12, 11, 14, 13, 16, 15, 18, 17]
LATTICE_WEIGHTS = [1.0 / 3.0] + [1.0 / 18.0] * 6 + [1.0 / 36.0] * 12
F32 = jnp.float32
BF16 = jnp.bfloat16
OUTSIDE = -100.0


def prep_kernel(inter_ref, pos_ref, anc_ref, cell_ref, w_ref, out_ref, tgt_ref, count_ref, force_ref):
    my_x, my_y, my_z = lax.axis_index("gx"), lax.axis_index("gy"), lax.axis_index("gz")

    def clear(b, carry):
        count_ref[b] = 0
        out_ref[b, 0:44] = jnp.zeros((44, VERT), F32)
        out_ref[b, 44:56] = jnp.full((12, VERT), OUTSIDE, F32)
        return carry

    lax.fori_loop(0, BRICKS, clear, 0)
    for c in range(3):
        pos = pos_ref[c]
        cycle = pltpu.roll(pos, 1, 1) + pltpu.roll(pos, VERT - 1, 1) - 2.0 * pos
        force_ref[c] = TENSION * cycle + TETHER * (anc_ref[c] - pos)

    def patch(p, carry):
        one = pl.ds(p, 1)
        weight = w_ref[p]
        force = [force_ref[c, one] for c in range(3)]
        x, y, z = cell_ref[0, one] - my_x * 16, cell_ref[1, one], cell_ref[2, one]
        for j in range(2):
            b = inter_ref[j, p]
            r = count_ref[b]
            count_ref[b] = r + 1
            by, bz = b // 4, b % 4
            away = (by - my_y + 8) % 8
            turn = jnp.where(away == 0, 0, jnp.where(away <= 4, 2 * away - 1, 2 * (8 - away)))
            tgt_ref[j, p] = (turn * 4 + (bz - my_z + 4) % 4) * SLOT_CAP + r
            local_y, local_z = y - by * 16, z - bz * 128
            inside = (x >= 0) & (x < 16) & (local_y >= 0) & (local_y < 16)
            inside = inside & (local_z >= 0) & (local_z < 128)
            out_ref[b, pl.ds(pl.multiple_of(r * 8, 8), 8)] = weight
            for a, coord in enumerate((x, local_y, local_z)):
                out_ref[b, pl.ds(32 + 4 * a + r, 1)] = force[a]
                out_ref[b, pl.ds(44 + 4 * a + r, 1)] = jnp.where(
                    inside, coord.astype(F32), OUTSIDE
                )
        return carry

    lax.fori_loop(0, PATCH_DEV, patch, 0)


def prep(intersection, positions, anchors, base_cell, weights):
    vmem = pl.BlockSpec(memory_space=pltpu.VMEM)
    smem = pl.BlockSpec(memory_space=pltpu.SMEM)
    return pl.pallas_call(
        prep_kernel,
        name="prep",
        out_shape=(
            jax.ShapeDtypeStruct((BRICKS, ROWS, VERT), F32),
            jax.ShapeDtypeStruct((2, PATCH_DEV), jnp.int32),
        ),
        in_specs=[smem, vmem, vmem, vmem, vmem],
        out_specs=(vmem, smem),
        scratch_shapes=[
            pltpu.SMEM((BRICKS,), jnp.int32),
            pltpu.VMEM((3, PATCH_DEV, VERT), F32),
        ],
    )(intersection, positions, anchors, base_cell, weights)


def halves(value):
    high = value.astype(BF16)
    return high, (value - high.astype(F32)).astype(BF16)


def scatter_factors(tab_ref, i, base_col, a_ref, z_ref):
    y_iota = lax.broadcasted_iota(jnp.int32, (16, VERT), 0).astype(F32)
    z_iota = lax.broadcasted_iota(jnp.int32, (256, VERT), 0).astype(F32)
    zero16 = jnp.zeros((16, VERT), BF16)
    for s in range(SLOT_CAP):
        x = tab_ref[i, pl.ds(44 + s, 1)]
        y = tab_ref[i, pl.ds(48 + s, 1)]
        z = tab_ref[i, pl.ds(52 + s, 1)]
        upper = x >= 8.0
        x_in = jnp.where(upper, x - 8.0, x)
        column = jnp.where(upper, z + 128.0, z)
        hot = jnp.where(z_iota == column, 1.0, 0.0).astype(BF16)
        for hl in range(2):
            z_ref[:, pl.ds(base_col + hl * 512 + s * VERT, VERT)] = hot
        at_y = y_iota == y
        at_y1 = y_iota - 1.0 == y
        x_wide = jnp.broadcast_to(x_in, (16, VERT)).astype(BF16)
        masks = [x_wide == jnp.asarray(k, BF16) for k in range(-1, 9)]
        for kz in range(2):
            for c in range(3):
                force = tab_ref[i, pl.ds(32 + 4 * c + s, 1)]
                parts = []
                for kx in range(2):
                    w0 = tab_ref[i, pl.ds(8 * s + 4 * kx + kz, 1)] * force
                    w1 = tab_ref[i, pl.ds(8 * s + 4 * kx + 2 + kz, 1)] * force
                    parts.append(halves(jnp.where(at_y, w0, jnp.where(at_y1, w1, 0.0))))
                base = (kz * 3 + c) * HALF
                for hl in range(2):
                    col = pl.ds(base_col + hl * 512 + s * VERT, VERT)
                    for plane in range(9):
                        a_ref[base + plane * 16 : base + plane * 16 + 16, col] = jnp.where(
                            masks[plane + 1],
                            parts[0][hl],
                            jnp.where(masks[plane], parts[1][hl], zero16),
                        )


def finish_force(acc_ref, force_ref):
    for c in range(3):
        for plane in range(16):
            pair = []
            for kz in range(2):
                base = (kz * 3 + c) * HALF
                if plane < 8:
                    total = acc_ref[base + plane * 16 : base + plane * 16 + 16, 0:128]
                elif plane == 8:
                    total = (
                        acc_ref[base + 128 : base + 144, 0:128]
                        + acc_ref[base : base + 16, 128:256]
                    )
                else:
                    start = base + (plane - 8) * 16
                    total = acc_ref[start : start + 16, 128:256]
                pair.append(total)
            force_ref[c, plane * 16 : plane * 16 + 16] = pair[0] + pltpu.roll(pair[1], 1, 1)


def collide_all(pop_ref, solid_ref, force_ref, post_ref, vel_ref):
    factor = 1.0 - 0.5 / RELAXATION

    def chunk(step, carry):
        x = step // 2
        yy = pl.ds(pl.multiple_of((step % 2) * 8, 8), 8)
        rows = pl.ds(pl.multiple_of(step * 8, 8), 8)
        pops = [pop_ref[q, x, yy] for q in range(19)]
        solid = solid_ref[x, yy] == 1
        force = [force_ref[c, rows] for c in range(3)]
        density = sum(pops[1:], pops[0])
        inverse = 1.0 / density
        velocity = []
        for a in range(3):
            plus = [pops[q] for q in range(19) if VELOCITIES[q][a] == 1]
            minus = [pops[q] for q in range(19) if VELOCITIES[q][a] == -1]
            momentum = sum(plus[1:], plus[0]) - sum(minus[1:], minus[0])
            u = (momentum + 0.5 * force[a]) * inverse
            velocity.append(u)
            vel_ref[a, rows] = u
        speed_sq = velocity[0] * velocity[0] + velocity[1] * velocity[1] + velocity[2] * velocity[2]
        u_dot_f = velocity[0] * force[0] + velocity[1] * force[1] + velocity[2] * force[2]
        common = 1.0 - 1.5 * speed_sq

        def along(direction, parts):
            total = None
            for step_a, part in zip(direction, parts):
                if step_a:
                    term = part if step_a == 1 else -part
                    total = term if total is None else total + term
            return total

        for q in range(19):
            w = LATTICE_WEIGHTS[q]
            if q == 0:
                equilibrium = w * density * common
                forcing = (factor * w) * (-3.0 * u_dot_f)
            else:
                along_u = along(VELOCITIES[q], velocity)
                along_f = along(VELOCITIES[q], force)
                equilibrium = w * density * (common + along_u * (3.0 + 4.5 * along_u))
                forcing = (factor * w) * (3.0 * (along_f - u_dot_f) + 9.0 * along_u * along_f)
            relaxed = pops[q] - (pops[q] - equilibrium) * (1.0 / RELAXATION) + forcing
            post_ref[q, x, yy] = jnp.where(solid, pops[OPPOSITE[q]], relaxed)
        return carry

    lax.fori_loop(0, 32, chunk, 0)


def transpose_velocity(vel_ref, vt_ref):
    for c in range(3):
        high, low = halves(vel_ref[c].T)
        rows = slice(c * 128, (c + 1) * 128)
        vt_ref[rows, 0:256] = high
        vt_ref[rows, 256:512] = high
        vt_ref[rows, 512:768] = low


def gather_chunk(tab_ref, i, b_ref, vt_ref, ret_ref):
    y_iota = lax.broadcasted_iota(jnp.int32, (16, VERT), 0).astype(F32)
    z_iota = lax.broadcasted_iota(jnp.int32, (VERT, VERT), 0).astype(F32)
    zero16 = jnp.zeros((16, VERT), BF16)
    for s in range(SLOT_CAP):
        x = tab_ref[i, pl.ds(44 + s, 1)]
        y = tab_ref[i, pl.ds(48 + s, 1)]
        z = tab_ref[i, pl.ds(52 + s, 1)]
        at_y = y_iota == y
        at_y1 = y_iota - 1.0 == y
        x_wide = jnp.broadcast_to(x, (16, VERT)).astype(BF16)
        masks = [x_wide == jnp.asarray(k, BF16) for k in range(-1, 16)]
        for kz in range(2):
            parts = []
            for kx in range(2):
                w0 = tab_ref[i, pl.ds(8 * s + 4 * kx + kz, 1)]
                w1 = tab_ref[i, pl.ds(8 * s + 4 * kx + 2 + kz, 1)]
                parts.append(halves(jnp.where(at_y, w0, jnp.where(at_y1, w1, 0.0))))
            cols = slice(kz * VERT, (kz + 1) * VERT)
            for hl in range(2):
                for plane in range(16):
                    value = jnp.where(
                        masks[plane + 1],
                        parts[0][hl],
                        jnp.where(masks[plane], parts[1][hl], zero16),
                    )
                    row = hl * 256 + plane * 16
                    b_ref[s, row : row + 16, cols] = value
                    if hl == 0:
                        b_ref[s, 512 + plane * 16 : 528 + plane * 16, cols] = value
        picked = jnp.dot(vt_ref[...], b_ref[s], preferred_element_type=F32)
        at_z = z_iota == z
        at_z1 = z_iota - 1.0 == z
        for c in range(3):
            rows = slice(c * 128, (c + 1) * 128)
            both = jnp.where(at_z, picked[rows, 0:128], 0.0) + jnp.where(
                at_z1, picked[rows, 128:256], 0.0
            )
            ret_ref[i, pl.ds(4 * c + s, 1)] = jnp.sum(both, axis=0, keepdims=True)


PLUS = [[q for q in range(19) if VELOCITIES[q][a] == 1] for a in range(3)]
MINUS = [[q for q in range(19) if VELOCITIES[q][a] == -1] for a in range(3)]
MESH = pl.DeviceIdType.MESH


def offset_of(i):
    j, dz = i // 4, i % 4
    half = (j + 1) // 2
    odd = j % 2
    return odd * half + (1 - odd) * ((8 - half) % 8), dz


def shift_x(post_ref, halo_ref):
    for k, q in enumerate(PLUS[0]):
        moved = post_ref[q, 0:15]
        post_ref[q, 1:16] = moved
        post_ref[q, 0] = halo_ref[0, k]
    for k, q in enumerate(MINUS[0]):
        moved = post_ref[q, 1:16]
        post_ref[q, 0:15] = moved
        post_ref[q, 15] = halo_ref[1, k]


def shift_y(post_ref, halo_ref):
    row = lax.broadcasted_iota(jnp.int32, (256, 128), 0) % 16
    for side, (directions, by, edge) in enumerate(((PLUS[1], 1, 0), (MINUS[1], 255, 15))):
        for k, q in enumerate(directions):
            moved = pltpu.roll(post_ref[q].reshape(256, 128), by, 0)
            halo = jnp.broadcast_to(halo_ref[side, k][:, None, :], (16, 16, 128)).reshape(256, 128)
            post_ref[q] = jnp.where(row == edge, halo, moved).reshape(16, 16, 128)


def turn_z(post_ref, send_ref):
    lane = lax.broadcasted_iota(jnp.int32, (256, 128), 1)
    for side, (directions, by, to) in enumerate(((PLUS[2], 1, 0), (MINUS[2], 127, 1))):
        packed = jnp.zeros((256, 128), F32)
        for k, q in enumerate(directions):
            moved = pltpu.roll(post_ref[q].reshape(256, 128), by, 1)
            post_ref[q] = moved.reshape(16, 16, 128)
            packed = jnp.where(lane == k, pltpu.roll(moved, k + to, 1) if k + to else moved, packed)
        send_ref[side] = packed


def shift_z(post_ref, halo_ref):
    lane = lax.broadcasted_iota(jnp.int32, (256, 128), 1)
    for side, (directions, edge) in enumerate(((PLUS[2], 0), (MINUS[2], 127))):
        packed = halo_ref[side]
        for k, q in enumerate(directions):
            by = (edge - k) % 128
            halo = pltpu.roll(packed, by, 1) if by else packed
            old = post_ref[q].reshape(256, 128)
            post_ref[q] = jnp.where(lane == edge, halo, old).reshape(16, 16, 128)


def step_kernel(
    out_ref, tgt_ref, pop_hbm, solid_hbm, read_hbm, vertex_ref,
    tab_ref, pop_ref, solid_ref, post_ref, a_ref, z_ref, acc_ref, force_ref, vel_ref, vt_ref, b_ref,
    ret_ref, back_ref, xs_ref, xr_ref, ys_ref, yr_ref, zs_ref, zr_ref,
    tab_send, tab_recv, ret_send, ret_recv, halo_send, halo_recv, load_sem, store_sem,
):
    my_x, my_y, my_z = lax.axis_index("gx"), lax.axis_index("gy"), lax.axis_index("gz")
    load_pop = pltpu.make_async_copy(pop_hbm, pop_ref, load_sem.at[0])
    load_solid = pltpu.make_async_copy(solid_hbm, solid_ref, load_sem.at[1])
    load_pop.start()
    load_solid.start()

    def ahead(i):
        dy, dz = offset_of(i)
        return (my_x, lax.rem(my_y + dy, 8), lax.rem(my_z + dz, 4))

    def behind(i):
        dy, dz = offset_of(i)
        return (my_x, lax.rem(my_y + 8 - dy, 8), lax.rem(my_z + 4 - dz, 4))

    up_x = (lax.rem(my_x + 1, 8), my_y, my_z)
    down_x = (lax.rem(my_x + 7, 8), my_y, my_z)
    up_y = (my_x, lax.rem(my_y + 1, 8), my_z)
    down_y = (my_x, lax.rem(my_y + 7, 8), my_z)
    up_z = (my_x, my_y, lax.rem(my_z + 1, 4))
    down_z = (my_x, my_y, lax.rem(my_z + 3, 4))

    barrier = pltpu.get_barrier_semaphore()

    def greet(i, carry):
        pl.semaphore_signal(barrier, inc=1, device_id=ahead(i), device_id_type=MESH)
        return carry

    lax.fori_loop(1, BRICKS, greet, 0)
    pl.semaphore_signal(barrier, inc=1, device_id=up_x, device_id_type=MESH)
    pl.semaphore_signal(barrier, inc=1, device_id=down_x, device_id_type=MESH)
    pl.semaphore_wait(barrier, BRICKS + 1)

    def table_copy(i):
        to = ahead(i)
        return pltpu.make_async_remote_copy(
            src_ref=out_ref.at[to[1] * 4 + to[2]],
            dst_ref=tab_ref.at[i],
            send_sem=tab_send.at[i],
            recv_sem=tab_recv.at[i],
            device_id=to,
            device_id_type=MESH,
        )

    def return_copy(i):
        return pltpu.make_async_remote_copy(
            src_ref=ret_ref.at[i],
            dst_ref=back_ref.at[i],
            send_sem=ret_send.at[i],
            recv_sem=ret_recv.at[i],
            device_id=behind(i),
            device_id_type=MESH,
        )

    def send_table(i, carry):
        table_copy(i).start()
        return carry

    lax.fori_loop(1, BRICKS, send_table, 0)
    tab_ref[0] = out_ref[my_y * 4 + my_z]
    acc_ref[...] = jnp.zeros_like(acc_ref)

    def scatter(t, carry):
        @pl.when(t > 0)
        def _():
            table_copy(2 * t).wait_recv()

        table_copy(2 * t + 1).wait_recv()
        for j in range(2):
            scatter_factors(tab_ref, 2 * t + j, j * 1024, a_ref, z_ref)
        acc_ref[...] += lax.dot_general(
            a_ref[...], z_ref[...], (((1,), (1,)), ((), ())), preferred_element_type=F32
        )
        return carry

    lax.fori_loop(0, BRICKS // 2, scatter, 0)
    finish_force(acc_ref, force_ref)
    load_pop.wait()
    load_solid.wait()
    collide_all(pop_ref, solid_ref, force_ref, post_ref, vel_ref)

    def halo_copy(k, src, dst, to):
        return pltpu.make_async_remote_copy(
            src_ref=src,
            dst_ref=dst,
            send_sem=halo_send.at[k],
            recv_sem=halo_recv.at[k],
            device_id=to,
            device_id_type=MESH,
        )

    halo = [
        halo_copy(0, xs_ref.at[0], xr_ref.at[0], up_x),
        halo_copy(1, xs_ref.at[1], xr_ref.at[1], down_x),
        halo_copy(2, ys_ref.at[0], yr_ref.at[0], up_y),
        halo_copy(3, ys_ref.at[1], yr_ref.at[1], down_y),
        halo_copy(4, zs_ref.at[0], zr_ref.at[0], up_z),
        halo_copy(5, zs_ref.at[1], zr_ref.at[1], down_z),
    ]
    for k in range(5):
        xs_ref[0, k] = post_ref[PLUS[0][k], 15]
        xs_ref[1, k] = post_ref[MINUS[0][k], 0]
    halo[0].start()
    halo[1].start()
    transpose_velocity(vel_ref, vt_ref)

    def store_copy(q):
        return pltpu.make_async_copy(post_ref.at[q], read_hbm.at[q], store_sem.at[q])

    along_z = PLUS[2] + MINUS[2]

    def gather(t, carry):
        for j in range(2):
            i = BRICKS - 1 - (2 * t + j)
            gather_chunk(tab_ref, i, b_ref, vt_ref, ret_ref)

            @pl.when(i > 0)
            def _():
                return_copy(i).start()

        @pl.when(t == 3)
        def _():
            halo[0].wait_recv()
            halo[1].wait_recv()
            shift_x(post_ref, xr_ref)
            for k in range(5):
                ys_ref[0, k] = post_ref[PLUS[1][k], :, 15, :]
                ys_ref[1, k] = post_ref[MINUS[1][k], :, 0, :]
            halo[2].start()
            halo[3].start()

        @pl.when(t == 7)
        def _():
            halo[2].wait_recv()
            halo[3].wait_recv()
            shift_y(post_ref, yr_ref)
            for q in range(19):
                if q not in along_z:
                    store_copy(q).start()
            turn_z(post_ref, zs_ref)
            halo[4].start()
            halo[5].start()

        @pl.when(t == 11)
        def _():
            halo[4].wait_recv()
            halo[5].wait_recv()
            shift_z(post_ref, zr_ref)
            for q in along_z:
                store_copy(q).start()

        return carry

    lax.fori_loop(0, BRICKS // 2, gather, 0)
    back_ref[0] = ret_ref[0]

    def wait_return(i, carry):
        return_copy(i).wait_recv()
        return carry

    lax.fori_loop(1, BRICKS, wait_return, 0)

    def patch(p, carry):
        first, second = tgt_ref[0, p], tgt_ref[1, p]
        for c in range(3):
            vertex_ref[c, pl.ds(p, 1)] = (
                back_ref[first // SLOT_CAP, pl.ds(4 * c + first % SLOT_CAP, 1)]
                + back_ref[second // SLOT_CAP, pl.ds(4 * c + second % SLOT_CAP, 1)]
            )
        return carry

    lax.fori_loop(0, PATCH_DEV, patch, 0)

    def wait_sends(i, carry):
        table_copy(i).wait_send()
        return_copy(i).wait_send()
        return carry

    lax.fori_loop(1, BRICKS, wait_sends, 0)
    for copy in halo:
        copy.wait_send()
    for q in range(19):
        store_copy(q).wait()


def step(outgoing, target, populations, solid_flags):
    vmem = pl.BlockSpec(memory_space=pltpu.VMEM)
    smem = pl.BlockSpec(memory_space=pltpu.SMEM)
    anywhere = pl.BlockSpec(memory_space=pl.ANY)
    dma = pltpu.SemaphoreType.DMA
    return pl.pallas_call(
        step_kernel,
        name="step",
        out_shape=(
            jax.ShapeDtypeStruct(populations.shape, F32),
            jax.ShapeDtypeStruct((3, PATCH_DEV, VERT), F32),
        ),
        in_specs=[vmem, smem, anywhere, anywhere],
        out_specs=(anywhere, vmem),
        scratch_shapes=[
            pltpu.VMEM((BRICKS, ROWS, VERT), F32),
            pltpu.VMEM((19, 16, 16, 128), F32),
            pltpu.VMEM((16, 16, 128), jnp.int32),
            pltpu.VMEM((19, 16, 16, 128), F32),
            pltpu.VMEM((6 * HALF, 2048), BF16),
            pltpu.VMEM((256, 2048), BF16),
            pltpu.VMEM((6 * HALF, 256), F32),
            pltpu.VMEM((3, 256, 128), F32),
            pltpu.VMEM((3, 256, 128), F32),
            pltpu.VMEM((384, 768), BF16),
            pltpu.VMEM((4, 768, 256), BF16),
            pltpu.VMEM((BRICKS, 12, VERT), F32),
            pltpu.VMEM((BRICKS, 12, VERT), F32),
            pltpu.VMEM((2, 5, 16, 128), F32),
            pltpu.VMEM((2, 5, 16, 128), F32),
            pltpu.VMEM((2, 5, 16, 128), F32),
            pltpu.VMEM((2, 5, 16, 128), F32),
            pltpu.VMEM((2, 256, 128), F32),
            pltpu.VMEM((2, 256, 128), F32),
            dma((BRICKS,)),
            dma((BRICKS,)),
            dma((BRICKS,)),
            dma((BRICKS,)),
            dma((6,)),
            dma((6,)),
            dma((2,)),
            dma((19,)),
        ],
        compiler_params=pltpu.CompilerParams(
            collective_id=0, has_side_effects=True, vmem_limit_bytes=40 * 1024 * 1024
        ),
    )(outgoing, target, populations, solid_flags)


def body(populations, solid_flags, positions, anchors, base_cell, weights, intersection):
    outgoing, target = prep(
        intersection.T,
        jnp.transpose(positions, (1, 0, 2)),
        jnp.transpose(anchors, (1, 0, 2)),
        jnp.transpose(base_cell, (1, 0, 2)),
        weights,
    )
    read, vertex = step(outgoing, target, populations, solid_flags)
    return (read, jnp.transpose(vertex, (1, 0, 2)))


def solution(mesh):
    return jax.shard_map(
        body,
        mesh=mesh,
        in_specs=(
            P(None, "gx", "gy", "gz"),
            P("gx", "gy", "gz"),
            P(("gx", "gy", "gz"), None, None),
            P(("gx", "gy", "gz"), None, None),
            P(("gx", "gy", "gz"), None, None),
            P(("gx", "gy", "gz"), None, None),
            P(("gx", "gy", "gz"), None),
        ),
        out_specs=(P(None, "gx", "gy", "gz"), P(("gx", "gy", "gz"), None, None)),
        check_vma=False,
    )
```

```python
import jax
import jax.numpy as jnp
from jax import lax
from jax.experimental import pallas as pl
from jax.experimental.pallas import tpu as pltpu
from jax.sharding import PartitionSpec as P

SLOT_CAP = 4
VERT = 128
BRICKS = 32
PATCH_DEV = 28
ROWS = 56
HALF = 9 * 16

RELAXATION = 0.8
TENSION = 0.05
TETHER = 0.5
VELOCITIES = [
    (0, 0, 0),
    (1, 0, 0),
    (-1, 0, 0),
    (0, 1, 0),
    (0, -1, 0),
    (0, 0, 1),
    (0, 0, -1),
    (1, 1, 0),
    (-1, -1, 0),
    (1, -1, 0),
    (-1, 1, 0),
    (1, 0, 1),
    (-1, 0, -1),
    (1, 0, -1),
    (-1, 0, 1),
    (0, 1, 1),
    (0, -1, -1),
    (0, 1, -1),
    (0, -1, 1),
]
LATTICE_WEIGHTS = [1.0 / 3.0] + [1.0 / 18.0] * 6 + [1.0 / 36.0] * 12
F32 = jnp.float32
BF16 = jnp.bfloat16
OUTSIDE = -100.0


def halves(value):
    high = value.astype(BF16)
    return high, (value - high.astype(F32)).astype(BF16)


def thirds(value):
    high = value.astype(BF16)
    rest = value - high.astype(F32)
    middle = rest.astype(BF16)
    return high, middle, (rest - middle.astype(F32)).astype(BF16)


def choose_slots(inter_ref, pad_ref, tgt_ref, my_y, my_z):
    pad_ref[...] = jnp.full((8, 128), -1, jnp.int32)
    tgt_ref[...] = jnp.zeros((8, 128), jnp.int32)
    pad_ref[0:2, 0:PATCH_DEV] = inter_ref[...]
    lane = lax.broadcasted_iota(jnp.int32, (BRICKS, 128), 1)
    brick_iota = lax.broadcasted_iota(jnp.int32, (BRICKS, 128), 0)
    rows = [pad_ref[j : j + 1] for j in range(2)]
    listed = [(brick_iota == row).astype(jnp.int32) for row in rows]
    total = listed[0] + listed[1]
    count = total
    for by in (1, 2, 4, 8, 16):
        count = count + jnp.where(lane >= by, pltpu.roll(count, by, 1), 0)
    before = count - total
    slots = []
    for j in range(2):
        rank = jnp.sum(listed[j] * before, axis=0, keepdims=True)
        slots.append(rows[j] * SLOT_CAP + rank)
        away = ((rows[j] >> 2) - my_y + 8) & 7
        turn = jnp.where(away == 0, 0, jnp.where(away <= 4, 2 * away - 1, 16 - 2 * away))
        side = ((rows[j] & 3) - my_z + 4) & 3
        tgt_ref[j : j + 1] = (turn * 4 + side) * SLOT_CAP + rank
    return slots


def make_tables(slots, pos_ref, anc_ref, cell_ref, w_ref, field_ref, part_ref, out_ref, my_x):
    field_ref[...] = jnp.zeros_like(field_ref)
    for k in range(8):
        field_ref[k, 0:PATCH_DEV] = w_ref[:, k, :]
    for c in range(3):
        pos = pos_ref[c]
        cycle = pltpu.roll(pos, 1, 1) + pltpu.roll(pos, VERT - 1, 1) - 2.0 * pos
        field_ref[8 + c, 0:PATCH_DEV] = TENSION * cycle + TETHER * (anc_ref[c] - pos)
        field_ref[11 + c, 0:PATCH_DEV] = cell_ref[c].astype(F32) + 1.0
    for f in range(14):
        for k, part in enumerate(thirds(field_ref[f])):
            part_ref[32 * k : 32 * k + 32, f * VERT : f * VERT + VERT] = part
    slot_iota = lax.broadcasted_iota(jnp.int32, (128, 128), 0)
    routed = (slot_iota == slots[0]) | (slot_iota == slots[1])
    routed = jnp.where(routed, 1.0, 0.0).astype(BF16)[:, 0:32]
    routed = jnp.concatenate([routed, routed, routed], axis=1)
    fields = [
        jnp.dot(routed, part_ref[:, f * VERT : f * VERT + VERT], preferred_element_type=F32)
        for f in range(14)
    ]
    brick = slot_iota // SLOT_CAP
    roots = (my_x * 16, (brick // 4) * 16, (brick % 4) * 128)
    cells = [fields[11 + a] - (1 + roots[a]).astype(F32) for a in range(3)]
    inside = None
    for cell, size in zip(cells, (16.0, 16.0, 128.0)):
        within = (cell >= 0.0) & (cell < size)
        inside = within if inside is None else inside & within
    for a in range(3):
        fields[11 + a] = jnp.where(inside, cells[a], OUTSIDE)
    low = slot_iota % 8 < 4
    for g in range(7):
        one, two = fields[2 * g], fields[2 * g + 1]
        even = jnp.where(low, one, pltpu.roll(two, 4, 0))
        odd = jnp.where(low, pltpu.roll(one, 124, 0), two)
        for m in range(16):
            out_ref[2 * m, 8 * g : 8 * g + 8] = even[8 * m : 8 * m + 8]
            out_ref[2 * m + 1, 8 * g : 8 * g + 8] = odd[8 * m : 8 * m + 8]


def scatter_factors(tab_ref, i, base_col, a_ref, z_ref):
    y_iota = lax.broadcasted_iota(jnp.int32, (16, VERT), 0).astype(F32)
    z_iota = lax.broadcasted_iota(jnp.int32, (256, VERT), 0).astype(F32)
    zero16 = jnp.zeros((16, VERT), BF16)
    for s in range(SLOT_CAP):
        x = tab_ref[i, pl.ds(44 + s, 1)]
        y = tab_ref[i, pl.ds(48 + s, 1)]
        z = tab_ref[i, pl.ds(52 + s, 1)]
        upper = x >= 8.0
        x_in = jnp.where(upper, x - 8.0, x)
        column = jnp.where(upper, z + 128.0, z)
        hot = jnp.where(z_iota == column, 1.0, 0.0).astype(BF16)
        for hl in range(2):
            z_ref[:, pl.ds(base_col + hl * 512 + s * VERT, VERT)] = hot
        at_y = y_iota == y
        at_y1 = y_iota - 1.0 == y
        x_wide = jnp.broadcast_to(x_in, (16, VERT)).astype(BF16)
        masks = [x_wide == jnp.asarray(k, BF16) for k in range(-1, 9)]
        for kz in range(2):
            for c in range(3):
                force = tab_ref[i, pl.ds(32 + 4 * c + s, 1)]
                parts = []
                for kx in range(2):
                    w0 = tab_ref[i, pl.ds(4 * (4 * kx + kz) + s, 1)] * force
                    w1 = tab_ref[i, pl.ds(4 * (4 * kx + 2 + kz) + s, 1)] * force
                    parts.append(halves(jnp.where(at_y, w0, jnp.where(at_y1, w1, 0.0))))
                base = (kz * 3 + c) * HALF
                for hl in range(2):
                    col = pl.ds(base_col + hl * 512 + s * VERT, VERT)
                    for plane in range(9):
                        a_ref[base + plane * 16 : base + plane * 16 + 16, col] = jnp.where(
                            masks[plane + 1],
                            parts[0][hl],
                            jnp.where(masks[plane], parts[1][hl], zero16),
                        )


def finish_force(acc_ref, force_ref):
    for c in range(3):
        for plane in range(16):
            pair = []
            for kz in range(2):
                base = (kz * 3 + c) * HALF
                if plane < 8:
                    total = acc_ref[base + plane * 16 : base + plane * 16 + 16, 0:128]
                elif plane == 8:
                    total = (
                        acc_ref[base + 128 : base + 144, 0:128]
                        + acc_ref[base : base + 16, 128:256]
                    )
                else:
                    start = base + (plane - 8) * 16
                    total = acc_ref[start : start + 16, 128:256]
                pair.append(total)
            force_ref[c, plane * 16 : plane * 16 + 16] = pair[0] + pltpu.roll(pair[1], 1, 1)


def collide_all(pop_ref, solid_ref, force_ref, post_ref, vel_ref):
    factor = 1.0 - 0.5 / RELAXATION

    def chunk(step, carry):
        x = step // 2
        yy = pl.ds(pl.multiple_of((step % 2) * 8, 8), 8)
        rows = pl.ds(pl.multiple_of(step * 8, 8), 8)
        pops = [pop_ref[q, x, yy] for q in range(19)]
        solid = solid_ref[x, yy] == 1
        force = [force_ref[c, rows] for c in range(3)]
        density = sum(pops[1:], pops[0])
        inverse = 1.0 / density
        velocity = []
        for a in range(3):
            plus = [pops[q] for q in range(19) if VELOCITIES[q][a] == 1]
            minus = [pops[q] for q in range(19) if VELOCITIES[q][a] == -1]
            momentum = sum(plus[1:], plus[0]) - sum(minus[1:], minus[0])
            u = (momentum + 0.5 * force[a]) * inverse
            velocity.append(u)
            vel_ref[a, rows] = u
        speed_sq = velocity[0] * velocity[0] + velocity[1] * velocity[1] + velocity[2] * velocity[2]
        u_dot_f = velocity[0] * force[0] + velocity[1] * force[1] + velocity[2] * force[2]
        rate = density * (1.0 / RELAXATION)
        common = rate * (1.0 - 1.5 * speed_sq) - (3.0 * factor) * u_dot_f
        square = [4.5 * rate * velocity[a] + (9.0 * factor) * force[a] for a in range(3)]
        linear = [3.0 * rate * velocity[a] + (3.0 * factor) * force[a] for a in range(3)]
        keep = 1.0 - 1.0 / RELAXATION

        def along(direction, parts):
            total = None
            for step_a, part in zip(direction, parts):
                if step_a:
                    term = part if step_a == 1 else -part
                    total = term if total is None else total + term
            return total

        relaxed = keep * pops[0] + LATTICE_WEIGHTS[0] * common
        post_ref[0, x, yy] = jnp.where(solid, pops[0], relaxed)
        for q in range(1, 19, 2):
            w = LATTICE_WEIGHTS[q]
            even = w * (common + along(VELOCITIES[q], velocity) * along(VELOCITIES[q], square))
            odd = w * along(VELOCITIES[q], linear)
            post_ref[q, x, yy] = jnp.where(solid, pops[q + 1], keep * pops[q] + (even + odd))
            post_ref[q + 1, x, yy] = jnp.where(solid, pops[q], keep * pops[q + 1] + (even - odd))
        return carry

    lax.fori_loop(0, 32, chunk, 0)


def transpose_velocity(vel_ref, vt_ref):
    for c in range(3):
        high, low = halves(vel_ref[c].T)
        rows = slice(c * 128, (c + 1) * 128)
        vt_ref[rows, 0:256] = high
        vt_ref[rows, 256:512] = high
        vt_ref[rows, 512:768] = low


def gather_chunk(tab_ref, i, b_ref, vt_ref, ret_ref):
    y_iota = lax.broadcasted_iota(jnp.int32, (16, VERT), 0).astype(F32)
    z_iota = lax.broadcasted_iota(jnp.int32, (VERT, VERT), 0).astype(F32)
    zero16 = jnp.zeros((16, VERT), BF16)
    for s in range(SLOT_CAP):
        x = tab_ref[i, pl.ds(44 + s, 1)]
        y = tab_ref[i, pl.ds(48 + s, 1)]
        z = tab_ref[i, pl.ds(52 + s, 1)]
        at_y = y_iota == y
        at_y1 = y_iota - 1.0 == y
        x_wide = jnp.broadcast_to(x, (16, VERT)).astype(BF16)
        masks = [x_wide == jnp.asarray(k, BF16) for k in range(-1, 16)]
        for kz in range(2):
            parts = []
            for kx in range(2):
                w0 = tab_ref[i, pl.ds(4 * (4 * kx + kz) + s, 1)]
                w1 = tab_ref[i, pl.ds(4 * (4 * kx + 2 + kz) + s, 1)]
                parts.append(halves(jnp.where(at_y, w0, jnp.where(at_y1, w1, 0.0))))
            cols = slice(kz * VERT, (kz + 1) * VERT)
            for hl in range(2):
                for plane in range(16):
                    value = jnp.where(
                        masks[plane + 1],
                        parts[0][hl],
                        jnp.where(masks[plane], parts[1][hl], zero16),
                    )
                    row = hl * 256 + plane * 16
                    b_ref[s, row : row + 16, cols] = value
                    if hl == 0:
                        b_ref[s, 512 + plane * 16 : 528 + plane * 16, cols] = value
        picked = jnp.dot(vt_ref[...], b_ref[s], preferred_element_type=F32)
        at_z = z_iota == z
        at_z1 = z_iota - 1.0 == z
        for c in range(3):
            rows = slice(c * 128, (c + 1) * 128)
            both = jnp.where(at_z, picked[rows, 0:128], 0.0) + jnp.where(
                at_z1, picked[rows, 128:256], 0.0
            )
            ret_ref[i, pl.ds(4 * c + s, 1)] = jnp.sum(both, axis=0, keepdims=True)


PLUS = [[q for q in range(19) if VELOCITIES[q][a] == 1] for a in range(3)]
MINUS = [[q for q in range(19) if VELOCITIES[q][a] == -1] for a in range(3)]
MESH = pl.DeviceIdType.MESH


def offset_of(i):
    j, dz = i // 4, i % 4
    half = (j + 1) // 2
    odd = j % 2
    return odd * half + (1 - odd) * ((8 - half) % 8), dz


def shift_x(post_ref, halo_ref):
    for k, q in enumerate(PLUS[0]):
        moved = post_ref[q, 0:15]
        post_ref[q, 1:16] = moved
        post_ref[q, 0] = halo_ref[0, k]
    for k, q in enumerate(MINUS[0]):
        moved = post_ref[q, 1:16]
        post_ref[q, 0:15] = moved
        post_ref[q, 15] = halo_ref[1, k]


def shift_y(post_ref, halo_ref):
    row = lax.broadcasted_iota(jnp.int32, (256, 128), 0) % 16
    for side, (directions, by, edge) in enumerate(((PLUS[1], 1, 0), (MINUS[1], 255, 15))):
        for k, q in enumerate(directions):
            moved = pltpu.roll(post_ref[q].reshape(256, 128), by, 0)
            halo = jnp.broadcast_to(halo_ref[side, k][:, None, :], (16, 16, 128)).reshape(256, 128)
            post_ref[q] = jnp.where(row == edge, halo, moved).reshape(16, 16, 128)


def turn_z(post_ref, send_ref):
    lane = lax.broadcasted_iota(jnp.int32, (256, 128), 1)
    for side, (directions, by, to) in enumerate(((PLUS[2], 1, 0), (MINUS[2], 127, 1))):
        packed = jnp.zeros((256, 128), F32)
        for k, q in enumerate(directions):
            moved = pltpu.roll(post_ref[q].reshape(256, 128), by, 1)
            post_ref[q] = moved.reshape(16, 16, 128)
            packed = jnp.where(lane == k, pltpu.roll(moved, k + to, 1) if k + to else moved, packed)
        send_ref[side] = packed


def shift_z(post_ref, halo_ref):
    lane = lax.broadcasted_iota(jnp.int32, (256, 128), 1)
    for side, (directions, edge) in enumerate(((PLUS[2], 0), (MINUS[2], 127))):
        packed = halo_ref[side]
        for k, q in enumerate(directions):
            by = (edge - k) % 128
            halo = pltpu.roll(packed, by, 1) if by else packed
            old = post_ref[q].reshape(256, 128)
            post_ref[q] = jnp.where(lane == edge, halo, old).reshape(16, 16, 128)


def step_kernel(
    inter_ref, pos_ref, anc_ref, cell_ref, w_ref, pop_hbm, solid_hbm, post_ref, vertex_ref,
    out_ref, tab_ref, pop_ref, solid_ref, a_ref, z_ref, acc_ref, force_ref, vel_ref, vt_ref, b_ref,
    ret_ref, back_ref, xs_ref, xr_ref, ys_ref, yr_ref, zs_ref, zr_ref, pad_ref, place_ref, tgt_ref,
    field_ref, part_ref, tab_send, tab_recv, ret_send, ret_recv, halo_send, halo_recv, load_sem,
):
    my_x, my_y, my_z = lax.axis_index("gx"), lax.axis_index("gy"), lax.axis_index("gz")
    load_pop = pltpu.make_async_copy(pop_hbm, pop_ref, load_sem.at[0])
    load_solid = pltpu.make_async_copy(solid_hbm, solid_ref, load_sem.at[1])
    load_target = pltpu.make_async_copy(place_ref, tgt_ref, load_sem.at[2])
    load_pop.start()
    load_solid.start()

    def ahead(i):
        dy, dz = offset_of(i)
        return (my_x, lax.rem(my_y + dy, 8), lax.rem(my_z + dz, 4))

    def behind(i):
        dy, dz = offset_of(i)
        return (my_x, lax.rem(my_y + 8 - dy, 8), lax.rem(my_z + 4 - dz, 4))

    up_x = (lax.rem(my_x + 1, 8), my_y, my_z)
    down_x = (lax.rem(my_x + 7, 8), my_y, my_z)
    up_y = (my_x, lax.rem(my_y + 1, 8), my_z)
    down_y = (my_x, lax.rem(my_y + 7, 8), my_z)
    up_z = (my_x, my_y, lax.rem(my_z + 1, 4))
    down_z = (my_x, my_y, lax.rem(my_z + 3, 4))

    barrier = pltpu.get_barrier_semaphore()

    def greet(i, carry):
        pl.semaphore_signal(barrier, inc=1, device_id=ahead(i), device_id_type=MESH)
        return carry

    lax.fori_loop(1, BRICKS, greet, 0)
    pl.semaphore_signal(barrier, inc=1, device_id=up_x, device_id_type=MESH)
    pl.semaphore_signal(barrier, inc=1, device_id=down_x, device_id_type=MESH)
    slots = choose_slots(inter_ref, pad_ref, place_ref, my_y, my_z)
    load_target.start()
    make_tables(slots, pos_ref, anc_ref, cell_ref, w_ref, field_ref, part_ref, out_ref, my_x)
    pl.semaphore_wait(barrier, BRICKS + 1)

    def table_copy(i):
        to = ahead(i)
        return pltpu.make_async_remote_copy(
            src_ref=out_ref.at[to[1] * 4 + to[2]],
            dst_ref=tab_ref.at[i],
            send_sem=tab_send.at[i],
            recv_sem=tab_recv.at[i],
            device_id=to,
            device_id_type=MESH,
        )

    def return_copy(i):
        return pltpu.make_async_remote_copy(
            src_ref=ret_ref.at[i],
            dst_ref=back_ref.at[i],
            send_sem=ret_send.at[i],
            recv_sem=ret_recv.at[i],
            device_id=behind(i),
            device_id_type=MESH,
        )

    def send_table(i, carry):
        table_copy(i).start()
        return carry

    lax.fori_loop(1, BRICKS, send_table, 0)
    tab_ref[0] = out_ref[my_y * 4 + my_z]
    acc_ref[...] = jnp.zeros_like(acc_ref)

    def scatter(t, carry):
        @pl.when(t > 0)
        def _():
            table_copy(2 * t).wait_recv()

        table_copy(2 * t + 1).wait_recv()
        for j in range(2):
            scatter_factors(tab_ref, 2 * t + j, j * 1024, a_ref, z_ref)
        acc_ref[...] += lax.dot_general(
            a_ref[...], z_ref[...], (((1,), (1,)), ((), ())), preferred_element_type=F32
        )
        return carry

    lax.fori_loop(0, BRICKS // 2, scatter, 0)
    finish_force(acc_ref, force_ref)
    load_pop.wait()
    load_solid.wait()
    collide_all(pop_ref, solid_ref, force_ref, post_ref, vel_ref)

    def halo_copy(k, src, dst, to):
        return pltpu.make_async_remote_copy(
            src_ref=src,
            dst_ref=dst,
            send_sem=halo_send.at[k],
            recv_sem=halo_recv.at[k],
            device_id=to,
            device_id_type=MESH,
        )

    halo = [
        halo_copy(0, xs_ref.at[0], xr_ref.at[0], up_x),
        halo_copy(1, xs_ref.at[1], xr_ref.at[1], down_x),
        halo_copy(2, ys_ref.at[0], yr_ref.at[0], up_y),
        halo_copy(3, ys_ref.at[1], yr_ref.at[1], down_y),
        halo_copy(4, zs_ref.at[0], zr_ref.at[0], up_z),
        halo_copy(5, zs_ref.at[1], zr_ref.at[1], down_z),
    ]
    for k in range(5):
        xs_ref[0, k] = post_ref[PLUS[0][k], 15]
        xs_ref[1, k] = post_ref[MINUS[0][k], 0]
    halo[0].start()
    halo[1].start()
    transpose_velocity(vel_ref, vt_ref)

    def gather(t, carry):
        for j in range(2):
            gather_chunk(tab_ref, BRICKS - 1 - (2 * t + j), b_ref.at[j], vt_ref, ret_ref)
        return_copy(BRICKS - 1 - 2 * t).start()

        @pl.when(t < BRICKS // 2 - 1)
        def _():
            return_copy(BRICKS - 2 - 2 * t).start()

        @pl.when(t == 3)
        def _():
            halo[0].wait_recv()
            halo[1].wait_recv()
            shift_x(post_ref, xr_ref)
            for k in range(5):
                ys_ref[0, k] = post_ref[PLUS[1][k], :, 15, :]
                ys_ref[1, k] = post_ref[MINUS[1][k], :, 0, :]
            halo[2].start()
            halo[3].start()

        @pl.when(t == 7)
        def _():
            halo[2].wait_recv()
            halo[3].wait_recv()
            shift_y(post_ref, yr_ref)
            turn_z(post_ref, zs_ref)
            halo[4].start()
            halo[5].start()

        @pl.when(t == 11)
        def _():
            halo[4].wait_recv()
            halo[5].wait_recv()
            shift_z(post_ref, zr_ref)

        return carry

    lax.fori_loop(0, BRICKS // 2, gather, 0)
    back_ref[0] = ret_ref[0]

    def wait_return(i, carry):
        return_copy(i).wait_recv()
        return carry

    lax.fori_loop(1, BRICKS, wait_return, 0)

    load_target.wait()

    def patch(p, carry):
        first = jnp.clip(tgt_ref[0, p], 0, BRICKS * SLOT_CAP - 1)
        second = jnp.clip(tgt_ref[1, p], 0, BRICKS * SLOT_CAP - 1)
        for c in range(3):
            vertex_ref[c, pl.ds(p, 1)] = (
                back_ref[first // SLOT_CAP, pl.ds(4 * c + first % SLOT_CAP, 1)]
                + back_ref[second // SLOT_CAP, pl.ds(4 * c + second % SLOT_CAP, 1)]
            )
        return carry

    lax.fori_loop(0, PATCH_DEV, patch, 0)

    def wait_sends(i, carry):
        table_copy(i).wait_send()
        return_copy(i).wait_send()
        return carry

    lax.fori_loop(1, BRICKS, wait_sends, 0)
    for copy in halo:
        copy.wait_send()


def step(intersection, positions, anchors, base_cell, weights, populations, solid_flags):
    vmem = pl.BlockSpec(memory_space=pltpu.VMEM)
    hbm = pl.BlockSpec(memory_space=pltpu.HBM)
    dma = pltpu.SemaphoreType.DMA
    return pl.pallas_call(
        step_kernel,
        name="step",
        out_shape=(
            jax.ShapeDtypeStruct(populations.shape, F32),
            jax.ShapeDtypeStruct((3, PATCH_DEV, VERT), F32),
        ),
        in_specs=[vmem, vmem, vmem, vmem, vmem, hbm, hbm],
        out_specs=(vmem, vmem),
        scratch_shapes=[
            pltpu.VMEM((BRICKS, ROWS, VERT), F32),
            pltpu.VMEM((BRICKS, ROWS, VERT), F32),
            pltpu.VMEM((19, 16, 16, 128), F32),
            pltpu.VMEM((16, 16, 128), jnp.int32),
            pltpu.VMEM((6 * HALF, 2048), BF16),
            pltpu.VMEM((256, 2048), BF16),
            pltpu.VMEM((6 * HALF, 256), F32),
            pltpu.VMEM((3, 256, 128), F32),
            pltpu.VMEM((3, 256, 128), F32),
            pltpu.VMEM((384, 768), BF16),
            pltpu.VMEM((2, 4, 768, 256), BF16),
            pltpu.VMEM((BRICKS, 12, VERT), F32),
            pltpu.VMEM((BRICKS, 12, VERT), F32),
            pltpu.VMEM((2, 5, 16, 128), F32),
            pltpu.VMEM((2, 5, 16, 128), F32),
            pltpu.VMEM((2, 5, 16, 128), F32),
            pltpu.VMEM((2, 5, 16, 128), F32),
            pltpu.VMEM((2, 256, 128), F32),
            pltpu.VMEM((2, 256, 128), F32),
            pltpu.VMEM((8, 128), jnp.int32),
            pltpu.VMEM((8, 128), jnp.int32),
            pltpu.SMEM((8, 128), jnp.int32),
            pltpu.VMEM((14, 32, VERT), F32),
            pltpu.VMEM((96, 14 * VERT), BF16),
            dma((BRICKS,)),
            dma((BRICKS,)),
            dma((BRICKS,)),
            dma((BRICKS,)),
            dma((6,)),
            dma((6,)),
            dma((3,)),
        ],
        compiler_params=pltpu.CompilerParams(
            collective_id=0, has_side_effects=True, vmem_limit_bytes=60 * 1024 * 1024
        ),
    )(intersection, positions, anchors, base_cell, weights, populations, solid_flags)


def body(populations, solid_flags, positions, anchors, base_cell, weights, intersection):
    read, vertex = step(
        intersection.T,
        jnp.transpose(positions, (1, 0, 2)),
        jnp.transpose(anchors, (1, 0, 2)),
        jnp.transpose(base_cell, (1, 0, 2)),
        weights,
        populations,
        solid_flags,
    )
    return (read, jnp.transpose(vertex, (1, 0, 2)))


def solution(mesh):
    return jax.shard_map(
        body,
        mesh=mesh,
        in_specs=(
            P(None, "gx", "gy", "gz"),
            P("gx", "gy", "gz"),
            P(("gx", "gy", "gz"), None, None),
            P(("gx", "gy", "gz"), None, None),
            P(("gx", "gy", "gz"), None, None),
            P(("gx", "gy", "gz"), None, None),
            P(("gx", "gy", "gz"), None),
        ),
        out_specs=(P(None, "gx", "gy", "gz"), P(("gx", "gy", "gz"), None, None)),
        check_vma=False,
    )
```

```python
import jax
import jax.numpy as jnp
from jax import lax
from jax.experimental import pallas as pl
from jax.experimental.pallas import tpu as pltpu
from jax.sharding import PartitionSpec as P

SLOT_CAP = 4
VERT = 128
BRICKS = 32
PATCH_DEV = 28
ROWS = 56
HALF = 9 * 16

RELAXATION = 0.8
TENSION = 0.05
TETHER = 0.5
VELOCITIES = [
    (0, 0, 0),
    (1, 0, 0),
    (-1, 0, 0),
    (0, 1, 0),
    (0, -1, 0),
    (0, 0, 1),
    (0, 0, -1),
    (1, 1, 0),
    (-1, -1, 0),
    (1, -1, 0),
    (-1, 1, 0),
    (1, 0, 1),
    (-1, 0, -1),
    (1, 0, -1),
    (-1, 0, 1),
    (0, 1, 1),
    (0, -1, -1),
    (0, 1, -1),
    (0, -1, 1),
]
LATTICE_WEIGHTS = [1.0 / 3.0] + [1.0 / 18.0] * 6 + [1.0 / 36.0] * 12
F32 = jnp.float32
BF16 = jnp.bfloat16
F8 = jnp.float8_e4m3fn
LOW_SCALE = 4096.0
TOP = 24.0
OUTSIDE = -100.0


def split(value):
    high = value.astype(BF16)
    return high, value - high.astype(F32)


def halves(value):
    high, low = split(value)
    return high, low.astype(BF16)


def thirds(value):
    high = value.astype(BF16)
    rest = value - high.astype(F32)
    middle = rest.astype(BF16)
    return high, middle, (rest - middle.astype(F32)).astype(BF16)


def choose_slots(inter_ref, pad_ref, tgt_ref, my_y, my_z):
    pad_ref[...] = jnp.full((8, 128), -1, jnp.int32)
    tgt_ref[...] = jnp.zeros((8, 128), jnp.int32)
    pad_ref[0:2, 0:PATCH_DEV] = inter_ref[...]
    lane = lax.broadcasted_iota(jnp.int32, (BRICKS, 128), 1)
    brick_iota = lax.broadcasted_iota(jnp.int32, (BRICKS, 128), 0)
    rows = [pad_ref[j : j + 1] for j in range(2)]
    listed = [(brick_iota == row).astype(jnp.int32) for row in rows]
    total = listed[0] + listed[1]
    count = total
    for by in (1, 2, 4, 8, 16):
        count = count + jnp.where(lane >= by, pltpu.roll(count, by, 1), 0)
    before = count - total
    slots = []
    for j in range(2):
        rank = jnp.sum(listed[j] * before, axis=0, keepdims=True)
        slots.append(rows[j] * SLOT_CAP + rank)
        away = ((rows[j] >> 2) - my_y + 8) & 7
        turn = jnp.where(away == 0, 0, jnp.where(away <= 4, 2 * away - 1, 16 - 2 * away))
        side = ((rows[j] & 3) - my_z + 4) & 3
        tgt_ref[j : j + 1] = (turn * 4 + side) * SLOT_CAP + rank
    return slots


def make_tables(slots, pos_ref, anc_ref, cell_ref, w_ref, field_ref, part_ref, out_ref, my_x):
    field_ref[...] = jnp.zeros_like(field_ref)
    for k in range(8):
        field_ref[k, 0:PATCH_DEV] = w_ref[:, k, :]
    for c in range(3):
        pos = pos_ref[c]
        cycle = pltpu.roll(pos, 1, 1) + pltpu.roll(pos, VERT - 1, 1) - 2.0 * pos
        field_ref[8 + c, 0:PATCH_DEV] = TENSION * cycle + TETHER * (anc_ref[c] - pos)
        field_ref[11 + c, 0:PATCH_DEV] = cell_ref[c].astype(F32) + 1.0
    for f in range(14):
        for k, part in enumerate(thirds(field_ref[f])):
            part_ref[32 * k : 32 * k + 32, f * VERT : f * VERT + VERT] = part
    slot_iota = lax.broadcasted_iota(jnp.int32, (128, 128), 0)
    routed = (slot_iota == slots[0]) | (slot_iota == slots[1])
    routed = jnp.where(routed, 1.0, 0.0).astype(BF16)[:, 0:32]
    routed = jnp.concatenate([routed, routed, routed], axis=1)
    fields = [
        jnp.dot(routed, part_ref[:, f * VERT : f * VERT + VERT], preferred_element_type=F32)
        for f in range(14)
    ]
    brick = slot_iota // SLOT_CAP
    roots = (my_x * 16, (brick // 4) * 16, (brick % 4) * 128)
    cells = [fields[11 + a] - (1 + roots[a]).astype(F32) for a in range(3)]
    inside = None
    for cell, size in zip(cells, (16.0, 16.0, 128.0)):
        within = (cell >= 0.0) & (cell < size)
        inside = within if inside is None else inside & within
    for a in range(3):
        fields[11 + a] = jnp.where(inside, cells[a], OUTSIDE)
    low = slot_iota % 8 < 4
    for g in range(7):
        one, two = fields[2 * g], fields[2 * g + 1]
        even = jnp.where(low, one, pltpu.roll(two, 4, 0))
        odd = jnp.where(low, pltpu.roll(one, 124, 0), two)
        for m in range(16):
            out_ref[2 * m, 8 * g : 8 * g + 8] = even[8 * m : 8 * m + 8]
            out_ref[2 * m + 1, 8 * g : 8 * g + 8] = odd[8 * m : 8 * m + 8]


def scatter_factors(tab_ref, i, base_col, a_ref, z_ref):
    y_iota = lax.broadcasted_iota(jnp.int32, (16, VERT), 0).astype(F32)
    z_iota = lax.broadcasted_iota(jnp.int32, (256, VERT), 0).astype(F32)
    zero16 = jnp.zeros((16, VERT), BF16)
    for s in range(SLOT_CAP):
        x = tab_ref[i, pl.ds(44 + s, 1)]
        y = tab_ref[i, pl.ds(48 + s, 1)]
        z = tab_ref[i, pl.ds(52 + s, 1)]
        upper = x >= 8.0
        x_in = jnp.where(upper, x - 8.0, x)
        column = jnp.where(upper, z + 128.0, z)
        hot = jnp.where(z_iota == column, 1.0, 0.0).astype(BF16)
        for hl in range(2):
            z_ref[:, pl.ds(base_col + hl * 512 + s * VERT, VERT)] = hot
        at_y = y_iota == y
        at_y1 = y_iota - 1.0 == y
        x_wide = jnp.broadcast_to(x_in, (16, VERT)).astype(BF16)
        masks = [x_wide == jnp.asarray(k, BF16) for k in range(-1, 9)]
        for kz in range(2):
            for c in range(3):
                force = tab_ref[i, pl.ds(32 + 4 * c + s, 1)]
                parts = []
                for kx in range(2):
                    w0 = tab_ref[i, pl.ds(4 * (4 * kx + kz) + s, 1)] * force
                    w1 = tab_ref[i, pl.ds(4 * (4 * kx + 2 + kz) + s, 1)] * force
                    parts.append(halves(jnp.where(at_y, w0, jnp.where(at_y1, w1, 0.0))))
                base = (kz * 3 + c) * HALF
                for hl in range(2):
                    col = pl.ds(base_col + hl * 512 + s * VERT, VERT)
                    for plane in range(9):
                        a_ref[base + plane * 16 : base + plane * 16 + 16, col] = jnp.where(
                            masks[plane + 1],
                            parts[0][hl],
                            jnp.where(masks[plane], parts[1][hl], zero16),
                        )


def finish_force(acc_ref, force_ref):
    for c in range(3):
        for plane in range(16):
            pair = []
            for kz in range(2):
                base = (kz * 3 + c) * HALF
                if plane < 8:
                    total = acc_ref[base + plane * 16 : base + plane * 16 + 16, 0:128]
                elif plane == 8:
                    total = (
                        acc_ref[base + 128 : base + 144, 0:128]
                        + acc_ref[base : base + 16, 128:256]
                    )
                else:
                    start = base + (plane - 8) * 16
                    total = acc_ref[start : start + 16, 128:256]
                pair.append(total)
            force_ref[c, plane * 16 : plane * 16 + 16] = pair[0] + pltpu.roll(pair[1], 1, 1)


def collide_all(pop_ref, solid_ref, force_ref, post_ref, vel_ref):
    factor = 1.0 - 0.5 / RELAXATION

    def chunk(step, carry):
        x = step // 2
        yy = pl.ds(pl.multiple_of((step % 2) * 8, 8), 8)
        rows = pl.ds(pl.multiple_of(step * 8, 8), 8)
        pops = [pop_ref[q, x, yy] for q in range(19)]
        solid = solid_ref[x, yy] == 1
        force = [force_ref[c, rows] for c in range(3)]
        density = sum(pops[1:], pops[0])
        inverse = 1.0 / density
        velocity, largest = [], carry
        for a in range(3):
            plus = [pops[q] for q in range(19) if VELOCITIES[q][a] == 1]
            minus = [pops[q] for q in range(19) if VELOCITIES[q][a] == -1]
            momentum = sum(plus[1:], plus[0]) - sum(minus[1:], minus[0])
            u = (momentum + 0.5 * force[a]) * inverse
            velocity.append(u)
            vel_ref[a, rows] = u
            largest = jnp.maximum(largest, jnp.abs(u))
        speed_sq = velocity[0] * velocity[0] + velocity[1] * velocity[1] + velocity[2] * velocity[2]
        u_dot_f = velocity[0] * force[0] + velocity[1] * force[1] + velocity[2] * force[2]
        rate = density * (1.0 / RELAXATION)
        common = rate * (1.0 - 1.5 * speed_sq) - (3.0 * factor) * u_dot_f
        square = [4.5 * rate * velocity[a] + (9.0 * factor) * force[a] for a in range(3)]
        linear = [3.0 * rate * velocity[a] + (3.0 * factor) * force[a] for a in range(3)]
        keep = 1.0 - 1.0 / RELAXATION

        def along(direction, parts):
            total = None
            for step_a, part in zip(direction, parts):
                if step_a:
                    term = part if step_a == 1 else -part
                    total = term if total is None else total + term
            return total

        relaxed = keep * pops[0] + LATTICE_WEIGHTS[0] * common
        post_ref[0, x, yy] = jnp.where(solid, pops[0], relaxed)
        for q in range(1, 19, 2):
            w = LATTICE_WEIGHTS[q]
            even = w * (common + along(VELOCITIES[q], velocity) * along(VELOCITIES[q], square))
            odd = w * along(VELOCITIES[q], linear)
            post_ref[q, x, yy] = jnp.where(solid, pops[q + 1], keep * pops[q] + (even + odd))
            post_ref[q + 1, x, yy] = jnp.where(solid, pops[q], keep * pops[q + 1] + (even - odd))
        return largest

    return lax.fori_loop(0, 32, chunk, jnp.zeros((8, 128), F32))


def transpose_velocity(vel_ref, largest, vt_ref, vt8_ref):
    largest = jnp.maximum(jnp.max(jnp.max(largest, axis=0, keepdims=True), axis=1, keepdims=True), 1e-30)
    scale = TOP / largest
    for c in range(3):
        high, low = split(vel_ref[c].T)
        rows = slice(c * 128, (c + 1) * 128)
        vt_ref[rows] = high
        vt8_ref[rows, 0:256] = (high.astype(F32) * scale).astype(F8)
        vt8_ref[rows, 256:512] = (low * (scale * LOW_SCALE)).astype(F8)
    return largest * (1.0 / (TOP * LOW_SCALE))


def gather_chunk(tab_ref, i, b_ref, b8_ref, vt_ref, vt8_ref, undo, ret_ref):
    y_iota = lax.broadcasted_iota(jnp.int32, (16, VERT), 0).astype(F32)
    z_iota = lax.broadcasted_iota(jnp.int32, (VERT, VERT), 0).astype(F32)
    zero16 = jnp.zeros((16, VERT), BF16)
    for s in range(SLOT_CAP):
        x = tab_ref[i, pl.ds(44 + s, 1)]
        y = tab_ref[i, pl.ds(48 + s, 1)]
        z = tab_ref[i, pl.ds(52 + s, 1)]
        at_y = y_iota == y
        at_y1 = y_iota - 1.0 == y
        x_wide = jnp.broadcast_to(x, (16, VERT)).astype(BF16)
        masks = [x_wide == jnp.asarray(k, BF16) for k in range(-1, 16)]
        for kz in range(2):
            parts = []
            for kx in range(2):
                w0 = tab_ref[i, pl.ds(4 * (4 * kx + kz) + s, 1)]
                w1 = tab_ref[i, pl.ds(4 * (4 * kx + 2 + kz) + s, 1)]
                high, low = split(jnp.where(at_y, w0, jnp.where(at_y1, w1, 0.0)))
                parts.append((high, (low * LOW_SCALE).astype(BF16)))
            cols = slice(kz * VERT, (kz + 1) * VERT)
            for hl in range(2):
                for pair in range(8):
                    planes = [
                        jnp.where(
                            masks[plane + 1],
                            parts[0][hl],
                            jnp.where(masks[plane], parts[1][hl], zero16),
                        )
                        for plane in (2 * pair, 2 * pair + 1)
                    ]
                    both = jnp.concatenate(planes, axis=0)
                    row = pair * 32
                    if hl == 0:
                        b_ref[s, row : row + 32, cols] = both
                    row = row + 256 * (1 - hl)
                    b8_ref[s, row : row + 32, cols] = both.astype(F8)
        picked = jnp.dot(vt_ref[...], b_ref[s], preferred_element_type=F32)
        picked = picked + undo * jnp.dot(vt8_ref[...], b8_ref[s], preferred_element_type=F32)
        at_z = z_iota == z
        at_z1 = z_iota - 1.0 == z
        for c in range(3):
            rows = slice(c * 128, (c + 1) * 128)
            both = jnp.where(at_z, picked[rows, 0:128], 0.0) + jnp.where(
                at_z1, picked[rows, 128:256], 0.0
            )
            ret_ref[i, pl.ds(4 * c + s, 1)] = jnp.sum(both, axis=0, keepdims=True)


PLUS = [[q for q in range(19) if VELOCITIES[q][a] == 1] for a in range(3)]
MINUS = [[q for q in range(19) if VELOCITIES[q][a] == -1] for a in range(3)]
MESH = pl.DeviceIdType.MESH


def offset_of(i):
    j, dz = i // 4, i % 4
    half = (j + 1) // 2
    odd = j % 2
    return odd * half + (1 - odd) * ((8 - half) % 8), dz


def shift_x(post_ref, halo_ref):
    for k, q in enumerate(PLUS[0]):
        moved = post_ref[q, 0:15]
        post_ref[q, 1:16] = moved
        post_ref[q, 0] = halo_ref[0, k]
    for k, q in enumerate(MINUS[0]):
        moved = post_ref[q, 1:16]
        post_ref[q, 0:15] = moved
        post_ref[q, 15] = halo_ref[1, k]


def shift_y(post_ref, halo_ref):
    row = lax.broadcasted_iota(jnp.int32, (256, 128), 0) % 16
    for side, (directions, by, edge) in enumerate(((PLUS[1], 1, 0), (MINUS[1], 255, 15))):
        for k, q in enumerate(directions):
            moved = pltpu.roll(post_ref[q].reshape(256, 128), by, 0)
            halo = jnp.broadcast_to(halo_ref[side, k][:, None, :], (16, 16, 128)).reshape(256, 128)
            post_ref[q] = jnp.where(row == edge, halo, moved).reshape(16, 16, 128)


def turn_z(post_ref, send_ref):
    lane = lax.broadcasted_iota(jnp.int32, (256, 128), 1)
    for side, (directions, by, to) in enumerate(((PLUS[2], 1, 0), (MINUS[2], 127, 1))):
        packed = jnp.zeros((256, 128), F32)
        for k, q in enumerate(directions):
            moved = pltpu.roll(post_ref[q].reshape(256, 128), by, 1)
            post_ref[q] = moved.reshape(16, 16, 128)
            packed = jnp.where(lane == k, pltpu.roll(moved, k + to, 1) if k + to else moved, packed)
        send_ref[side] = packed


def shift_z(post_ref, halo_ref):
    lane = lax.broadcasted_iota(jnp.int32, (256, 128), 1)
    for side, (directions, edge) in enumerate(((PLUS[2], 0), (MINUS[2], 127))):
        packed = halo_ref[side]
        for k, q in enumerate(directions):
            by = (edge - k) % 128
            halo = pltpu.roll(packed, by, 1) if by else packed
            old = post_ref[q].reshape(256, 128)
            post_ref[q] = jnp.where(lane == edge, halo, old).reshape(16, 16, 128)


def step_kernel(
    inter_ref, pos_ref, anc_ref, cell_ref, w_ref, pop_hbm, solid_hbm, post_ref, vertex_ref,
    out_ref, tab_ref, pop_ref, solid_ref, a_ref, z_ref, acc_ref, force_ref, vel_ref, vt_ref, vt8_ref, b_ref, b8_ref,
    ret_ref, back_ref, xs_ref, xr_ref, ys_ref, yr_ref, zs_ref, zr_ref, pad_ref, place_ref, tgt_ref,
    field_ref, part_ref, tab_send, tab_recv, ret_send, ret_recv, halo_send, halo_recv, load_sem,
):
    my_x, my_y, my_z = lax.axis_index("gx"), lax.axis_index("gy"), lax.axis_index("gz")
    load_pop = pltpu.make_async_copy(pop_hbm, pop_ref, load_sem.at[0])
    load_solid = pltpu.make_async_copy(solid_hbm, solid_ref, load_sem.at[1])
    load_target = pltpu.make_async_copy(place_ref, tgt_ref, load_sem.at[2])
    load_pop.start()
    load_solid.start()

    def ahead(i):
        dy, dz = offset_of(i)
        return (my_x, lax.rem(my_y + dy, 8), lax.rem(my_z + dz, 4))

    def behind(i):
        dy, dz = offset_of(i)
        return (my_x, lax.rem(my_y + 8 - dy, 8), lax.rem(my_z + 4 - dz, 4))

    up_x = (lax.rem(my_x + 1, 8), my_y, my_z)
    down_x = (lax.rem(my_x + 7, 8), my_y, my_z)
    up_y = (my_x, lax.rem(my_y + 1, 8), my_z)
    down_y = (my_x, lax.rem(my_y + 7, 8), my_z)
    up_z = (my_x, my_y, lax.rem(my_z + 1, 4))
    down_z = (my_x, my_y, lax.rem(my_z + 3, 4))

    barrier = pltpu.get_barrier_semaphore()

    def greet(i, carry):
        pl.semaphore_signal(barrier, inc=1, device_id=ahead(i), device_id_type=MESH)
        return carry

    lax.fori_loop(1, BRICKS, greet, 0)
    pl.semaphore_signal(barrier, inc=1, device_id=up_x, device_id_type=MESH)
    pl.semaphore_signal(barrier, inc=1, device_id=down_x, device_id_type=MESH)
    slots = choose_slots(inter_ref, pad_ref, place_ref, my_y, my_z)
    load_target.start()
    make_tables(slots, pos_ref, anc_ref, cell_ref, w_ref, field_ref, part_ref, out_ref, my_x)
    pl.semaphore_wait(barrier, BRICKS + 1)

    def table_copy(i):
        to = ahead(i)
        return pltpu.make_async_remote_copy(
            src_ref=out_ref.at[to[1] * 4 + to[2]],
            dst_ref=tab_ref.at[i],
            send_sem=tab_send.at[i],
            recv_sem=tab_recv.at[i],
            device_id=to,
            device_id_type=MESH,
        )

    def return_copy(i):
        return pltpu.make_async_remote_copy(
            src_ref=ret_ref.at[i],
            dst_ref=back_ref.at[i],
            send_sem=ret_send.at[i],
            recv_sem=ret_recv.at[i],
            device_id=behind(i),
            device_id_type=MESH,
        )

    def send_table(i, carry):
        table_copy(i).start()
        return carry

    lax.fori_loop(1, BRICKS, send_table, 0)
    tab_ref[0] = out_ref[my_y * 4 + my_z]
    acc_ref[...] = jnp.zeros_like(acc_ref)

    def scatter(t, carry):
        @pl.when(t > 0)
        def _():
            table_copy(2 * t).wait_recv()

        table_copy(2 * t + 1).wait_recv()
        for j in range(2):
            scatter_factors(tab_ref, 2 * t + j, j * 1024, a_ref, z_ref)
        acc_ref[...] += lax.dot_general(
            a_ref[...], z_ref[...], (((1,), (1,)), ((), ())), preferred_element_type=F32
        )
        return carry

    lax.fori_loop(0, BRICKS // 2, scatter, 0)
    finish_force(acc_ref, force_ref)
    load_pop.wait()
    load_solid.wait()
    largest = collide_all(pop_ref, solid_ref, force_ref, post_ref, vel_ref)

    def halo_copy(k, src, dst, to):
        return pltpu.make_async_remote_copy(
            src_ref=src,
            dst_ref=dst,
            send_sem=halo_send.at[k],
            recv_sem=halo_recv.at[k],
            device_id=to,
            device_id_type=MESH,
        )

    halo = [
        halo_copy(0, xs_ref.at[0], xr_ref.at[0], up_x),
        halo_copy(1, xs_ref.at[1], xr_ref.at[1], down_x),
        halo_copy(2, ys_ref.at[0], yr_ref.at[0], up_y),
        halo_copy(3, ys_ref.at[1], yr_ref.at[1], down_y),
        halo_copy(4, zs_ref.at[0], zr_ref.at[0], up_z),
        halo_copy(5, zs_ref.at[1], zr_ref.at[1], down_z),
    ]
    for k in range(5):
        xs_ref[0, k] = post_ref[PLUS[0][k], 15]
        xs_ref[1, k] = post_ref[MINUS[0][k], 0]
    halo[0].start()
    halo[1].start()
    undo = transpose_velocity(vel_ref, largest, vt_ref, vt8_ref)

    def gather(t, carry):
        for j in range(2):
            i = BRICKS - 1 - (2 * t + j)
            gather_chunk(tab_ref, i, b_ref.at[j], b8_ref.at[j], vt_ref, vt8_ref, undo, ret_ref)
        return_copy(BRICKS - 1 - 2 * t).start()

        @pl.when(t < BRICKS // 2 - 1)
        def _():
            return_copy(BRICKS - 2 - 2 * t).start()

        @pl.when(t == 3)
        def _():
            halo[0].wait_recv()
            halo[1].wait_recv()
            shift_x(post_ref, xr_ref)
            for k in range(5):
                ys_ref[0, k] = post_ref[PLUS[1][k], :, 15, :]
                ys_ref[1, k] = post_ref[MINUS[1][k], :, 0, :]
            halo[2].start()
            halo[3].start()

        @pl.when(t == 7)
        def _():
            halo[2].wait_recv()
            halo[3].wait_recv()
            shift_y(post_ref, yr_ref)
            turn_z(post_ref, zs_ref)
            halo[4].start()
            halo[5].start()

        @pl.when(t == 11)
        def _():
            halo[4].wait_recv()
            halo[5].wait_recv()
            shift_z(post_ref, zr_ref)

        return carry

    lax.fori_loop(0, BRICKS // 2, gather, 0)
    back_ref[0] = ret_ref[0]

    def wait_return(i, carry):
        return_copy(i).wait_recv()
        return carry

    lax.fori_loop(1, BRICKS, wait_return, 0)

    load_target.wait()

    def patch(p, carry):
        first = jnp.clip(tgt_ref[0, p], 0, BRICKS * SLOT_CAP - 1)
        second = jnp.clip(tgt_ref[1, p], 0, BRICKS * SLOT_CAP - 1)
        for c in range(3):
            vertex_ref[c, pl.ds(p, 1)] = (
                back_ref[first // SLOT_CAP, pl.ds(4 * c + first % SLOT_CAP, 1)]
                + back_ref[second // SLOT_CAP, pl.ds(4 * c + second % SLOT_CAP, 1)]
            )
        return carry

    lax.fori_loop(0, PATCH_DEV, patch, 0)

    def wait_sends(i, carry):
        table_copy(i).wait_send()
        return_copy(i).wait_send()
        return carry

    lax.fori_loop(1, BRICKS, wait_sends, 0)
    for copy in halo:
        copy.wait_send()


def step(intersection, positions, anchors, base_cell, weights, populations, solid_flags):
    vmem = pl.BlockSpec(memory_space=pltpu.VMEM)
    hbm = pl.BlockSpec(memory_space=pltpu.HBM)
    dma = pltpu.SemaphoreType.DMA
    return pl.pallas_call(
        step_kernel,
        name="step",
        out_shape=(
            jax.ShapeDtypeStruct(populations.shape, F32),
            jax.ShapeDtypeStruct((3, PATCH_DEV, VERT), F32),
        ),
        in_specs=[vmem, vmem, vmem, vmem, vmem, hbm, hbm],
        out_specs=(vmem, vmem),
        scratch_shapes=[
            pltpu.VMEM((BRICKS, ROWS, VERT), F32),
            pltpu.VMEM((BRICKS, ROWS, VERT), F32),
            pltpu.VMEM((19, 16, 16, 128), F32),
            pltpu.VMEM((16, 16, 128), jnp.int32),
            pltpu.VMEM((6 * HALF, 2048), BF16),
            pltpu.VMEM((256, 2048), BF16),
            pltpu.VMEM((6 * HALF, 256), F32),
            pltpu.VMEM((3, 256, 128), F32),
            pltpu.VMEM((3, 256, 128), F32),
            pltpu.VMEM((384, 256), BF16),
            pltpu.VMEM((384, 512), F8),
            pltpu.VMEM((2, 4, 256, 256), BF16),
            pltpu.VMEM((2, 4, 512, 256), F8),
            pltpu.VMEM((BRICKS, 12, VERT), F32),
            pltpu.VMEM((BRICKS, 12, VERT), F32),
            pltpu.VMEM((2, 5, 16, 128), F32),
            pltpu.VMEM((2, 5, 16, 128), F32),
            pltpu.VMEM((2, 5, 16, 128), F32),
            pltpu.VMEM((2, 5, 16, 128), F32),
            pltpu.VMEM((2, 256, 128), F32),
            pltpu.VMEM((2, 256, 128), F32),
            pltpu.VMEM((8, 128), jnp.int32),
            pltpu.VMEM((8, 128), jnp.int32),
            pltpu.SMEM((8, 128), jnp.int32),
            pltpu.VMEM((14, 32, VERT), F32),
            pltpu.VMEM((96, 14 * VERT), BF16),
            dma((BRICKS,)),
            dma((BRICKS,)),
            dma((BRICKS,)),
            dma((BRICKS,)),
            dma((6,)),
            dma((6,)),
            dma((3,)),
        ],
        compiler_params=pltpu.CompilerParams(
            collective_id=0, has_side_effects=True, vmem_limit_bytes=60 * 1024 * 1024
        ),
    )(intersection, positions, anchors, base_cell, weights, populations, solid_flags)


def body(populations, solid_flags, positions, anchors, base_cell, weights, intersection):
    read, vertex = step(
        intersection.T,
        jnp.transpose(positions, (1, 0, 2)),
        jnp.transpose(anchors, (1, 0, 2)),
        jnp.transpose(base_cell, (1, 0, 2)),
        weights,
        populations,
        solid_flags,
    )
    return (read, jnp.transpose(vertex, (1, 0, 2)))


def solution(mesh):
    return jax.shard_map(
        body,
        mesh=mesh,
        in_specs=(
            P(None, "gx", "gy", "gz"),
            P("gx", "gy", "gz"),
            P(("gx", "gy", "gz"), None, None),
            P(("gx", "gy", "gz"), None, None),
            P(("gx", "gy", "gz"), None, None),
            P(("gx", "gy", "gz"), None, None),
            P(("gx", "gy", "gz"), None),
        ),
        out_specs=(P(None, "gx", "gy", "gz"), P(("gx", "gy", "gz"), None, None)),
        check_vma=False,
    )
```

```python
import jax
import jax.numpy as jnp
from jax import lax
from jax.experimental import pallas as pl
from jax.experimental.pallas import tpu as pltpu
from jax.sharding import PartitionSpec as P

SLOT_CAP = 4
VERT = 128
BRICKS = 32
PATCH_DEV = 28
ROWS = 56
HALF = 9 * 16

RELAXATION = 0.8
TENSION = 0.05
TETHER = 0.5
VELOCITIES = [
    (0, 0, 0),
    (1, 0, 0),
    (-1, 0, 0),
    (0, 1, 0),
    (0, -1, 0),
    (0, 0, 1),
    (0, 0, -1),
    (1, 1, 0),
    (-1, -1, 0),
    (1, -1, 0),
    (-1, 1, 0),
    (1, 0, 1),
    (-1, 0, -1),
    (1, 0, -1),
    (-1, 0, 1),
    (0, 1, 1),
    (0, -1, -1),
    (0, 1, -1),
    (0, -1, 1),
]
LATTICE_WEIGHTS = [1.0 / 3.0] + [1.0 / 18.0] * 6 + [1.0 / 36.0] * 12
F32 = jnp.float32
BF16 = jnp.bfloat16
F8 = jnp.float8_e4m3fn
LOW_SCALE = 4096.0
TOP = 24.0
OUTSIDE = -100.0


def split(value):
    high = value.astype(BF16)
    return high, value - high.astype(F32)


def thirds(value):
    high = value.astype(BF16)
    rest = value - high.astype(F32)
    middle = rest.astype(BF16)
    return high, middle, (rest - middle.astype(F32)).astype(BF16)


def choose_slots(inter_ref, pad_ref, tgt_ref, my_y, my_z):
    pad_ref[...] = jnp.full((8, 128), -1, jnp.int32)
    tgt_ref[...] = jnp.zeros((8, 128), jnp.int32)
    pad_ref[0:2, 0:PATCH_DEV] = inter_ref[...]
    lane = lax.broadcasted_iota(jnp.int32, (BRICKS, 128), 1)
    brick_iota = lax.broadcasted_iota(jnp.int32, (BRICKS, 128), 0)
    rows = [pad_ref[j : j + 1] for j in range(2)]
    listed = [(brick_iota == row).astype(jnp.int32) for row in rows]
    total = listed[0] + listed[1]
    count = total
    for by in (1, 2, 4, 8, 16):
        count = count + jnp.where(lane >= by, pltpu.roll(count, by, 1), 0)
    before = count - total
    slots = []
    for j in range(2):
        rank = jnp.sum(listed[j] * before, axis=0, keepdims=True)
        slots.append(rows[j] * SLOT_CAP + rank)
        away = ((rows[j] >> 2) - my_y + 8) & 7
        turn = jnp.where(away == 0, 0, jnp.where(away <= 4, 2 * away - 1, 16 - 2 * away))
        side = ((rows[j] & 3) - my_z + 4) & 3
        tgt_ref[j : j + 1] = (turn * 4 + side) * SLOT_CAP + rank
    return slots


def make_tables(slots, pos_ref, anc_ref, cell_ref, w_ref, field_ref, part_ref, out_ref, my_x):
    field_ref[...] = jnp.zeros_like(field_ref)
    for k in range(8):
        field_ref[k, 0:PATCH_DEV] = w_ref[:, k, :]
    for c in range(3):
        pos = pos_ref[c]
        cycle = pltpu.roll(pos, 1, 1) + pltpu.roll(pos, VERT - 1, 1) - 2.0 * pos
        field_ref[8 + c, 0:PATCH_DEV] = TENSION * cycle + TETHER * (anc_ref[c] - pos)
        field_ref[11 + c, 0:PATCH_DEV] = cell_ref[c].astype(F32) + 1.0
    for f in range(14):
        for k, part in enumerate(thirds(field_ref[f])):
            part_ref[32 * k : 32 * k + 32, f * VERT : f * VERT + VERT] = part
    slot_iota = lax.broadcasted_iota(jnp.int32, (128, 128), 0)
    routed = (slot_iota == slots[0]) | (slot_iota == slots[1])
    routed = jnp.where(routed, 1.0, 0.0).astype(BF16)[:, 0:32]
    routed = jnp.concatenate([routed, routed, routed], axis=1)
    fields = [
        jnp.dot(routed, part_ref[:, f * VERT : f * VERT + VERT], preferred_element_type=F32)
        for f in range(14)
    ]
    brick = slot_iota // SLOT_CAP
    roots = (my_x * 16, (brick // 4) * 16, (brick % 4) * 128)
    cells = [fields[11 + a] - (1 + roots[a]).astype(F32) for a in range(3)]
    inside = None
    for cell, size in zip(cells, (16.0, 16.0, 128.0)):
        within = (cell >= 0.0) & (cell < size)
        inside = within if inside is None else inside & within
    for a in range(3):
        fields[11 + a] = jnp.where(inside, cells[a], OUTSIDE)
    low = slot_iota % 8 < 4
    for g in range(7):
        one, two = fields[2 * g], fields[2 * g + 1]
        even = jnp.where(low, one, pltpu.roll(two, 4, 0))
        odd = jnp.where(low, pltpu.roll(one, 124, 0), two)
        for m in range(16):
            out_ref[2 * m, 8 * g : 8 * g + 8] = even[8 * m : 8 * m + 8]
            out_ref[2 * m + 1, 8 * g : 8 * g + 8] = odd[8 * m : 8 * m + 8]


def scatter_factors(tab_ref, i, base_col, a_ref, a8_ref, z_ref, z8_ref):
    y_iota = lax.broadcasted_iota(jnp.int32, (16, VERT), 0).astype(F32)
    z_iota = lax.broadcasted_iota(jnp.int32, (256, VERT), 0).astype(F32).astype(BF16)
    zero16 = jnp.zeros((16, VERT), BF16)
    ones = jnp.ones((256, VERT), BF16)
    zeros = jnp.zeros((256, VERT), BF16)
    for s in range(SLOT_CAP):
        x = tab_ref[i, pl.ds(44 + s, 1)]
        y = tab_ref[i, pl.ds(48 + s, 1)]
        z = tab_ref[i, pl.ds(52 + s, 1)]
        upper = x >= 8.0
        x_in = jnp.where(upper, x - 8.0, x)
        column = jnp.where(upper, z + 128.0, z)
        col = slice(base_col + s * VERT, base_col + (s + 1) * VERT)
        hot = jnp.where(
            z_iota == jnp.broadcast_to(column, (256, VERT)).astype(BF16), ones, zeros
        )
        z_ref[:, col] = hot
        z8_ref[:, col] = hot.astype(F8)
        at_y = y_iota == y
        at_y1 = y_iota - 1.0 == y
        x_wide = jnp.broadcast_to(x_in, (16, VERT)).astype(BF16)
        masks = [x_wide == jnp.asarray(k, BF16) for k in range(-1, 9)]
        for pair in range(3):
            blocks = []
            for kz, c in (divmod(2 * pair, 3), divmod(2 * pair + 1, 3)):
                force = tab_ref[i, pl.ds(32 + 4 * c + s, 1)]
                parts = []
                for kx in range(2):
                    w0 = tab_ref[i, pl.ds(4 * (4 * kx + kz) + s, 1)] * force
                    w1 = tab_ref[i, pl.ds(4 * (4 * kx + 2 + kz) + s, 1)] * force
                    high, low = split(jnp.where(at_y, w0, jnp.where(at_y1, w1, 0.0)))
                    parts.append((high, (low * LOW_SCALE).astype(BF16)))
                for plane in range(9):
                    blocks.append(
                        [
                            jnp.where(
                                masks[plane + 1],
                                parts[0][hl],
                                jnp.where(masks[plane], parts[1][hl], zero16),
                            )
                            for hl in range(2)
                        ]
                    )
            for n in range(9):
                rows = slice(pair * 2 * HALF + n * 32, pair * 2 * HALF + n * 32 + 32)
                first, second = blocks[2 * n], blocks[2 * n + 1]
                a_ref[rows, col] = jnp.concatenate([first[0], second[0]], axis=0)
                a8_ref[rows, col] = jnp.concatenate([first[1], second[1]], axis=0).astype(F8)


def finish_force(acc_ref, force_ref):
    for c in range(3):
        for plane in range(16):
            pair = []
            for kz in range(2):
                base = (kz * 3 + c) * HALF
                if plane < 8:
                    total = acc_ref[base + plane * 16 : base + plane * 16 + 16, 0:128]
                elif plane == 8:
                    total = (
                        acc_ref[base + 128 : base + 144, 0:128]
                        + acc_ref[base : base + 16, 128:256]
                    )
                else:
                    start = base + (plane - 8) * 16
                    total = acc_ref[start : start + 16, 128:256]
                pair.append(total)
            force_ref[c, plane * 16 : plane * 16 + 16] = pair[0] + pltpu.roll(pair[1], 1, 1)


def collide_all(pop_ref, solid_ref, force_ref, post_ref, vel_ref):
    factor = 1.0 - 0.5 / RELAXATION

    def chunk(step, carry):
        x = step // 2
        yy = pl.ds(pl.multiple_of((step % 2) * 8, 8), 8)
        rows = pl.ds(pl.multiple_of(step * 8, 8), 8)
        pops = [pop_ref[q, x, yy] for q in range(19)]
        solid = solid_ref[x, yy] == 1
        force = [force_ref[c, rows] for c in range(3)]
        density = sum(pops[1:], pops[0])
        inverse = 1.0 / density
        velocity, largest = [], carry
        for a in range(3):
            plus = [pops[q] for q in range(19) if VELOCITIES[q][a] == 1]
            minus = [pops[q] for q in range(19) if VELOCITIES[q][a] == -1]
            momentum = sum(plus[1:], plus[0]) - sum(minus[1:], minus[0])
            u = (momentum + 0.5 * force[a]) * inverse
            velocity.append(u)
            vel_ref[a, rows] = u
            largest = jnp.maximum(largest, jnp.abs(u))
        speed_sq = velocity[0] * velocity[0] + velocity[1] * velocity[1] + velocity[2] * velocity[2]
        u_dot_f = velocity[0] * force[0] + velocity[1] * force[1] + velocity[2] * force[2]
        rate = density * (1.0 / RELAXATION)
        common = rate * (1.0 - 1.5 * speed_sq) - (3.0 * factor) * u_dot_f
        square = [4.5 * rate * velocity[a] + (9.0 * factor) * force[a] for a in range(3)]
        linear = [3.0 * rate * velocity[a] + (3.0 * factor) * force[a] for a in range(3)]
        keep = 1.0 - 1.0 / RELAXATION

        def along(direction, parts):
            total = None
            for step_a, part in zip(direction, parts):
                if step_a:
                    term = part if step_a == 1 else -part
                    total = term if total is None else total + term
            return total

        relaxed = keep * pops[0] + LATTICE_WEIGHTS[0] * common
        post_ref[0, x, yy] = jnp.where(solid, pops[0], relaxed)
        for q in range(1, 19, 2):
            w = LATTICE_WEIGHTS[q]
            even = w * (common + along(VELOCITIES[q], velocity) * along(VELOCITIES[q], square))
            odd = w * along(VELOCITIES[q], linear)
            post_ref[q, x, yy] = jnp.where(solid, pops[q + 1], keep * pops[q] + (even + odd))
            post_ref[q + 1, x, yy] = jnp.where(solid, pops[q], keep * pops[q + 1] + (even - odd))
        return largest

    return lax.fori_loop(0, 32, chunk, jnp.zeros((8, 128), F32))


def transpose_velocity(vel_ref, largest, vt_ref, vt8_ref):
    largest = jnp.maximum(jnp.max(jnp.max(largest, axis=0, keepdims=True), axis=1, keepdims=True), 1e-30)
    scale = TOP / largest
    for c in range(3):
        high, low = split(vel_ref[c].T)
        rows = slice(c * 128, (c + 1) * 128)
        vt_ref[rows] = high
        vt8_ref[rows, 0:256] = (high.astype(F32) * scale).astype(F8)
        vt8_ref[rows, 256:512] = (low * (scale * LOW_SCALE)).astype(F8)
    return largest * (1.0 / (TOP * LOW_SCALE))


def gather_chunk(tab_ref, i, b_ref, b8_ref, vt_ref, vt8_ref, undo, ret_ref):
    y_iota = lax.broadcasted_iota(jnp.int32, (16, VERT), 0).astype(F32)
    z_iota = lax.broadcasted_iota(jnp.int32, (VERT, VERT), 0).astype(F32)
    zero16 = jnp.zeros((16, VERT), BF16)
    for s in range(SLOT_CAP):
        x = tab_ref[i, pl.ds(44 + s, 1)]
        y = tab_ref[i, pl.ds(48 + s, 1)]
        z = tab_ref[i, pl.ds(52 + s, 1)]
        at_y = y_iota == y
        at_y1 = y_iota - 1.0 == y
        x_wide = jnp.broadcast_to(x, (16, VERT)).astype(BF16)
        masks = [x_wide == jnp.asarray(k, BF16) for k in range(-1, 16)]
        for kz in range(2):
            parts = []
            for kx in range(2):
                w0 = tab_ref[i, pl.ds(4 * (4 * kx + kz) + s, 1)]
                w1 = tab_ref[i, pl.ds(4 * (4 * kx + 2 + kz) + s, 1)]
                high, low = split(jnp.where(at_y, w0, jnp.where(at_y1, w1, 0.0)))
                parts.append((high, (low * LOW_SCALE).astype(BF16)))
            cols = slice(kz * VERT, (kz + 1) * VERT)
            for hl in range(2):
                for pair in range(8):
                    planes = [
                        jnp.where(
                            masks[plane + 1],
                            parts[0][hl],
                            jnp.where(masks[plane], parts[1][hl], zero16),
                        )
                        for plane in (2 * pair, 2 * pair + 1)
                    ]
                    both = jnp.concatenate(planes, axis=0)
                    row = pair * 32
                    if hl == 0:
                        b_ref[s, row : row + 32, cols] = both
                    row = row + 256 * (1 - hl)
                    b8_ref[s, row : row + 32, cols] = both.astype(F8)
        picked = jnp.dot(vt_ref[...], b_ref[s], preferred_element_type=F32)
        picked = picked + undo * jnp.dot(vt8_ref[...], b8_ref[s], preferred_element_type=F32)
        at_z = z_iota == z
        at_z1 = z_iota - 1.0 == z
        for c in range(3):
            rows = slice(c * 128, (c + 1) * 128)
            both = jnp.where(at_z, picked[rows, 0:128], 0.0) + jnp.where(
                at_z1, picked[rows, 128:256], 0.0
            )
            ret_ref[i, pl.ds(4 * c + s, 1)] = jnp.sum(both, axis=0, keepdims=True)


PLUS = [[q for q in range(19) if VELOCITIES[q][a] == 1] for a in range(3)]
MINUS = [[q for q in range(19) if VELOCITIES[q][a] == -1] for a in range(3)]
MESH = pl.DeviceIdType.MESH


def offset_of(i):
    j, dz = i // 4, i % 4
    half = (j + 1) // 2
    odd = j % 2
    return odd * half + (1 - odd) * ((8 - half) % 8), dz


def shift_x(post_ref, halo_ref):
    for k, q in enumerate(PLUS[0]):
        moved = post_ref[q, 0:15]
        post_ref[q, 1:16] = moved
        post_ref[q, 0] = halo_ref[0, k]
    for k, q in enumerate(MINUS[0]):
        moved = post_ref[q, 1:16]
        post_ref[q, 0:15] = moved
        post_ref[q, 15] = halo_ref[1, k]


def shift_y(post_ref, halo_ref):
    row = lax.broadcasted_iota(jnp.int32, (256, 128), 0) % 16
    for side, (directions, by, edge) in enumerate(((PLUS[1], 1, 0), (MINUS[1], 255, 15))):
        for k, q in enumerate(directions):
            moved = pltpu.roll(post_ref[q].reshape(256, 128), by, 0)
            halo = jnp.broadcast_to(halo_ref[side, k][:, None, :], (16, 16, 128)).reshape(256, 128)
            post_ref[q] = jnp.where(row == edge, halo, moved).reshape(16, 16, 128)


def turn_z(post_ref, send_ref):
    lane = lax.broadcasted_iota(jnp.int32, (256, 128), 1)
    for side, (directions, by, to) in enumerate(((PLUS[2], 1, 0), (MINUS[2], 127, 1))):
        packed = jnp.zeros((256, 128), F32)
        for k, q in enumerate(directions):
            moved = pltpu.roll(post_ref[q].reshape(256, 128), by, 1)
            post_ref[q] = moved.reshape(16, 16, 128)
            packed = jnp.where(lane == k, pltpu.roll(moved, k + to, 1) if k + to else moved, packed)
        send_ref[side] = packed


def shift_z(post_ref, halo_ref):
    lane = lax.broadcasted_iota(jnp.int32, (256, 128), 1)
    for side, (directions, edge) in enumerate(((PLUS[2], 0), (MINUS[2], 127))):
        packed = halo_ref[side]
        for k, q in enumerate(directions):
            by = (edge - k) % 128
            halo = pltpu.roll(packed, by, 1) if by else packed
            old = post_ref[q].reshape(256, 128)
            post_ref[q] = jnp.where(lane == edge, halo, old).reshape(16, 16, 128)


def step_kernel(
    inter_ref, pos_ref, anc_ref, cell_ref, w_ref, pop_hbm, solid_hbm, read_hbm, vertex_ref,
    out_ref, tab_ref, pop_ref, solid_ref, post_ref, a_ref, a8_ref, z_ref, z8_ref, acc_ref, force_ref, vel_ref, vt_ref, vt8_ref, b_ref, b8_ref,
    ret_ref, back_ref, xs_ref, xr_ref, ys_ref, yr_ref, zs_ref, zr_ref, pad_ref, place_ref, tgt_ref,
    field_ref, part_ref, tab_send, tab_recv, ret_send, ret_recv, halo_send, halo_recv, load_sem, store_sem,
):
    my_x, my_y, my_z = lax.axis_index("gx"), lax.axis_index("gy"), lax.axis_index("gz")
    load_pop = pltpu.make_async_copy(pop_hbm, pop_ref, load_sem.at[0])
    load_solid = pltpu.make_async_copy(solid_hbm, solid_ref, load_sem.at[1])
    load_target = pltpu.make_async_copy(place_ref, tgt_ref, load_sem.at[2])
    load_pop.start()
    load_solid.start()

    def ahead(i):
        dy, dz = offset_of(i)
        return (my_x, lax.rem(my_y + dy, 8), lax.rem(my_z + dz, 4))

    def behind(i):
        dy, dz = offset_of(i)
        return (my_x, lax.rem(my_y + 8 - dy, 8), lax.rem(my_z + 4 - dz, 4))

    up_x = (lax.rem(my_x + 1, 8), my_y, my_z)
    down_x = (lax.rem(my_x + 7, 8), my_y, my_z)
    up_y = (my_x, lax.rem(my_y + 1, 8), my_z)
    down_y = (my_x, lax.rem(my_y + 7, 8), my_z)
    up_z = (my_x, my_y, lax.rem(my_z + 1, 4))
    down_z = (my_x, my_y, lax.rem(my_z + 3, 4))

    barrier = pltpu.get_barrier_semaphore()

    def greet(i, carry):
        pl.semaphore_signal(barrier, inc=1, device_id=ahead(i), device_id_type=MESH)
        return carry

    lax.fori_loop(1, BRICKS, greet, 0)
    pl.semaphore_signal(barrier, inc=1, device_id=up_x, device_id_type=MESH)
    pl.semaphore_signal(barrier, inc=1, device_id=down_x, device_id_type=MESH)
    slots = choose_slots(inter_ref, pad_ref, place_ref, my_y, my_z)
    load_target.start()
    make_tables(slots, pos_ref, anc_ref, cell_ref, w_ref, field_ref, part_ref, out_ref, my_x)
    pl.semaphore_wait(barrier, BRICKS + 1)

    def table_copy(i):
        to = ahead(i)
        return pltpu.make_async_remote_copy(
            src_ref=out_ref.at[to[1] * 4 + to[2]],
            dst_ref=tab_ref.at[i],
            send_sem=tab_send.at[i],
            recv_sem=tab_recv.at[i],
            device_id=to,
            device_id_type=MESH,
        )

    def return_copy(i):
        return pltpu.make_async_remote_copy(
            src_ref=ret_ref.at[i],
            dst_ref=back_ref.at[i],
            send_sem=ret_send.at[i],
            recv_sem=ret_recv.at[i],
            device_id=behind(i),
            device_id_type=MESH,
        )

    def send_table(i, carry):
        table_copy(i).start()
        return carry

    lax.fori_loop(1, BRICKS, send_table, 0)
    tab_ref[0] = out_ref[my_y * 4 + my_z]
    acc_ref[...] = jnp.zeros_like(acc_ref)

    def scatter(t, carry):
        @pl.when(t > 0)
        def _():
            table_copy(2 * t).wait_recv()

        table_copy(2 * t + 1).wait_recv()
        for j in range(2):
            scatter_factors(tab_ref, 2 * t + j, j * 512, a_ref, a8_ref, z_ref, z8_ref)
        dims = (((1,), (1,)), ((), ()))
        high = lax.dot_general(a_ref[...], z_ref[...], dims, preferred_element_type=F32)
        low = lax.dot_general(a8_ref[...], z8_ref[...], dims, preferred_element_type=F32)
        acc_ref[...] += high + low * (1.0 / LOW_SCALE)
        return carry

    lax.fori_loop(0, BRICKS // 2, scatter, 0)
    finish_force(acc_ref, force_ref)
    load_pop.wait()
    load_solid.wait()
    largest = collide_all(pop_ref, solid_ref, force_ref, post_ref, vel_ref)

    def halo_copy(k, src, dst, to):
        return pltpu.make_async_remote_copy(
            src_ref=src,
            dst_ref=dst,
            send_sem=halo_send.at[k],
            recv_sem=halo_recv.at[k],
            device_id=to,
            device_id_type=MESH,
        )

    halo = [
        halo_copy(0, xs_ref.at[0], xr_ref.at[0], up_x),
        halo_copy(1, xs_ref.at[1], xr_ref.at[1], down_x),
        halo_copy(2, ys_ref.at[0], yr_ref.at[0], up_y),
        halo_copy(3, ys_ref.at[1], yr_ref.at[1], down_y),
        halo_copy(4, zs_ref.at[0], zr_ref.at[0], up_z),
        halo_copy(5, zs_ref.at[1], zr_ref.at[1], down_z),
    ]
    for k in range(5):
        xs_ref[0, k] = post_ref[PLUS[0][k], 15]
        xs_ref[1, k] = post_ref[MINUS[0][k], 0]
    halo[0].start()
    halo[1].start()
    undo = transpose_velocity(vel_ref, largest, vt_ref, vt8_ref)

    def store_copy(q):
        return pltpu.make_async_copy(post_ref.at[q], read_hbm.at[q], store_sem.at[q])

    along_z = PLUS[2] + MINUS[2]

    def gather(t, carry):
        for j in range(2):
            i = BRICKS - 1 - (2 * t + j)
            gather_chunk(tab_ref, i, b_ref.at[j], b8_ref.at[j], vt_ref, vt8_ref, undo, ret_ref)
        return_copy(BRICKS - 1 - 2 * t).start()

        @pl.when(t < BRICKS // 2 - 1)
        def _():
            return_copy(BRICKS - 2 - 2 * t).start()

        @pl.when(t == 3)
        def _():
            halo[0].wait_recv()
            halo[1].wait_recv()
            shift_x(post_ref, xr_ref)
            for k in range(5):
                ys_ref[0, k] = post_ref[PLUS[1][k], :, 15, :]
                ys_ref[1, k] = post_ref[MINUS[1][k], :, 0, :]
            halo[2].start()
            halo[3].start()

        @pl.when(t == 7)
        def _():
            halo[2].wait_recv()
            halo[3].wait_recv()
            shift_y(post_ref, yr_ref)
            for q in range(19):
                if q not in along_z:
                    store_copy(q).start()
            turn_z(post_ref, zs_ref)
            halo[4].start()
            halo[5].start()

        @pl.when(t == 11)
        def _():
            halo[4].wait_recv()
            halo[5].wait_recv()
            shift_z(post_ref, zr_ref)
            for q in along_z:
                store_copy(q).start()

        return carry

    lax.fori_loop(0, BRICKS // 2, gather, 0)
    back_ref[0] = ret_ref[0]

    def wait_return(i, carry):
        return_copy(i).wait_recv()
        return carry

    lax.fori_loop(1, BRICKS, wait_return, 0)

    load_target.wait()

    def patch(p, carry):
        first = jnp.clip(tgt_ref[0, p], 0, BRICKS * SLOT_CAP - 1)
        second = jnp.clip(tgt_ref[1, p], 0, BRICKS * SLOT_CAP - 1)
        for c in range(3):
            vertex_ref[c, pl.ds(p, 1)] = (
                back_ref[first // SLOT_CAP, pl.ds(4 * c + first % SLOT_CAP, 1)]
                + back_ref[second // SLOT_CAP, pl.ds(4 * c + second % SLOT_CAP, 1)]
            )
        return carry

    lax.fori_loop(0, PATCH_DEV, patch, 0)

    def wait_sends(i, carry):
        table_copy(i).wait_send()
        return_copy(i).wait_send()
        return carry

    lax.fori_loop(1, BRICKS, wait_sends, 0)
    for copy in halo:
        copy.wait_send()
    for q in range(19):
        store_copy(q).wait()


def step(intersection, positions, anchors, base_cell, weights, populations, solid_flags):
    vmem = pl.BlockSpec(memory_space=pltpu.VMEM)
    hbm = pl.BlockSpec(memory_space=pltpu.HBM)
    dma = pltpu.SemaphoreType.DMA
    return pl.pallas_call(
        step_kernel,
        name="step",
        out_shape=(
            jax.ShapeDtypeStruct(populations.shape, F32),
            jax.ShapeDtypeStruct((3, PATCH_DEV, VERT), F32),
        ),
        in_specs=[vmem, vmem, vmem, vmem, vmem, hbm, hbm],
        out_specs=(hbm, vmem),
        scratch_shapes=[
            pltpu.VMEM((BRICKS, ROWS, VERT), F32),
            pltpu.VMEM((BRICKS, ROWS, VERT), F32),
            pltpu.VMEM((19, 16, 16, 128), F32),
            pltpu.VMEM((16, 16, 128), jnp.int32),
            pltpu.VMEM((19, 16, 16, 128), F32),
            pltpu.VMEM((6 * HALF, 1024), BF16),
            pltpu.VMEM((6 * HALF, 1024), F8),
            pltpu.VMEM((256, 1024), BF16),
            pltpu.VMEM((256, 1024), F8),
            pltpu.VMEM((6 * HALF, 256), F32),
            pltpu.VMEM((3, 256, 128), F32),
            pltpu.VMEM((3, 256, 128), F32),
            pltpu.VMEM((384, 256), BF16),
            pltpu.VMEM((384, 512), F8),
            pltpu.VMEM((2, 4, 256, 256), BF16),
            pltpu.VMEM((2, 4, 512, 256), F8),
            pltpu.VMEM((BRICKS, 12, VERT), F32),
            pltpu.VMEM((BRICKS, 12, VERT), F32),
            pltpu.VMEM((2, 5, 16, 128), F32),
            pltpu.VMEM((2, 5, 16, 128), F32),
            pltpu.VMEM((2, 5, 16, 128), F32),
            pltpu.VMEM((2, 5, 16, 128), F32),
            pltpu.VMEM((2, 256, 128), F32),
            pltpu.VMEM((2, 256, 128), F32),
            pltpu.VMEM((8, 128), jnp.int32),
            pltpu.VMEM((8, 128), jnp.int32),
            pltpu.SMEM((8, 128), jnp.int32),
            pltpu.VMEM((14, 32, VERT), F32),
            pltpu.VMEM((96, 14 * VERT), BF16),
            dma((BRICKS,)),
            dma((BRICKS,)),
            dma((BRICKS,)),
            dma((BRICKS,)),
            dma((6,)),
            dma((6,)),
            dma((3,)),
            dma((19,)),
        ],
        compiler_params=pltpu.CompilerParams(
            collective_id=0, has_side_effects=True, vmem_limit_bytes=60 * 1024 * 1024
        ),
    )(intersection, positions, anchors, base_cell, weights, populations, solid_flags)


def body(populations, solid_flags, positions, anchors, base_cell, weights, intersection):
    read, vertex = step(
        intersection.T,
        jnp.transpose(positions, (1, 0, 2)),
        jnp.transpose(anchors, (1, 0, 2)),
        jnp.transpose(base_cell, (1, 0, 2)),
        weights,
        populations,
        solid_flags,
    )
    return (read, jnp.transpose(vertex, (1, 0, 2)))


def solution(mesh):
    return jax.shard_map(
        body,
        mesh=mesh,
        in_specs=(
            P(None, "gx", "gy", "gz"),
            P("gx", "gy", "gz"),
            P(("gx", "gy", "gz"), None, None),
            P(("gx", "gy", "gz"), None, None),
            P(("gx", "gy", "gz"), None, None),
            P(("gx", "gy", "gz"), None, None),
            P(("gx", "gy", "gz"), None),
        ),
        out_specs=(P(None, "gx", "gy", "gz"), P(("gx", "gy", "gz"), None, None)),
        check_vma=False,
    )
```

```python
import jax
import jax.numpy as jnp
from jax import lax
from jax.experimental import pallas as pl
from jax.experimental.pallas import tpu as pltpu
from jax.sharding import PartitionSpec as P

SLOT_CAP = 4
VERT = 128
BRICKS = 32
PATCH_DEV = 28
ROWS = 56
HALF = 9 * 16

RELAXATION = 0.8
TENSION = 0.05
TETHER = 0.5
VELOCITIES = [
    (0, 0, 0),
    (1, 0, 0),
    (-1, 0, 0),
    (0, 1, 0),
    (0, -1, 0),
    (0, 0, 1),
    (0, 0, -1),
    (1, 1, 0),
    (-1, -1, 0),
    (1, -1, 0),
    (-1, 1, 0),
    (1, 0, 1),
    (-1, 0, -1),
    (1, 0, -1),
    (-1, 0, 1),
    (0, 1, 1),
    (0, -1, -1),
    (0, 1, -1),
    (0, -1, 1),
]
LATTICE_WEIGHTS = [1.0 / 3.0] + [1.0 / 18.0] * 6 + [1.0 / 36.0] * 12
F32 = jnp.float32
BF16 = jnp.bfloat16
F8 = jnp.float8_e4m3fn
LOW_SCALE = 4096.0
TOP = 24.0
OUTSIDE = -100.0


def split(value):
    high = value.astype(BF16)
    return high, value - high.astype(F32)


def thirds(value):
    high = value.astype(BF16)
    rest = value - high.astype(F32)
    middle = rest.astype(BF16)
    return high, middle, (rest - middle.astype(F32)).astype(BF16)


def choose_slots(inter_ref, pad_ref, tgt_ref, my_y, my_z):
    pad_ref[...] = jnp.full((8, 128), -1, jnp.int32)
    tgt_ref[...] = jnp.zeros((8, 128), jnp.int32)
    pad_ref[0:2, 0:PATCH_DEV] = inter_ref[...]
    lane = lax.broadcasted_iota(jnp.int32, (BRICKS, 128), 1)
    brick_iota = lax.broadcasted_iota(jnp.int32, (BRICKS, 128), 0)
    rows = [pad_ref[j : j + 1] for j in range(2)]
    listed = [(brick_iota == row).astype(jnp.int32) for row in rows]
    total = listed[0] + listed[1]
    count = total
    for by in (1, 2, 4, 8, 16):
        count = count + jnp.where(lane >= by, pltpu.roll(count, by, 1), 0)
    before = count - total
    slots = []
    for j in range(2):
        rank = jnp.sum(listed[j] * before, axis=0, keepdims=True)
        slots.append(rows[j] * SLOT_CAP + rank)
        away = ((rows[j] >> 2) - my_y + 8) & 7
        turn = jnp.where(away == 0, 0, jnp.where(away <= 4, 2 * away - 1, 16 - 2 * away))
        side = ((rows[j] & 3) - my_z + 4) & 3
        tgt_ref[j : j + 1] = (turn * 4 + side) * SLOT_CAP + rank
    return slots


def make_tables(slots, pos_ref, anc_ref, cell_ref, w_ref, field_ref, part_ref, out_ref, my_x):
    field_ref[...] = jnp.zeros_like(field_ref)
    for k in range(8):
        field_ref[k, 0:PATCH_DEV] = w_ref[:, k, :]
    for c in range(3):
        pos = pos_ref[c]
        cycle = pltpu.roll(pos, 1, 1) + pltpu.roll(pos, VERT - 1, 1) - 2.0 * pos
        field_ref[8 + c, 0:PATCH_DEV] = TENSION * cycle + TETHER * (anc_ref[c] - pos)
        field_ref[11 + c, 0:PATCH_DEV] = cell_ref[c].astype(F32) + 1.0
    for f in range(14):
        for k, part in enumerate(thirds(field_ref[f])):
            part_ref[32 * k : 32 * k + 32, f * VERT : f * VERT + VERT] = part
    slot_iota = lax.broadcasted_iota(jnp.int32, (128, 128), 0)
    routed = (slot_iota == slots[0]) | (slot_iota == slots[1])
    routed = jnp.where(routed, 1.0, 0.0).astype(BF16)[:, 0:32]
    routed = jnp.concatenate([routed, routed, routed], axis=1)
    fields = [
        jnp.dot(routed, part_ref[:, f * VERT : f * VERT + VERT], preferred_element_type=F32)
        for f in range(14)
    ]
    brick = slot_iota // SLOT_CAP
    roots = (my_x * 16, (brick // 4) * 16, (brick % 4) * 128)
    cells = [fields[11 + a] - (1 + roots[a]).astype(F32) for a in range(3)]
    inside = None
    for cell, size in zip(cells, (16.0, 16.0, 128.0)):
        within = (cell >= 0.0) & (cell < size)
        inside = within if inside is None else inside & within
    for a in range(3):
        fields[11 + a] = jnp.where(inside, cells[a], OUTSIDE)
    low = slot_iota % 8 < 4
    for g in range(7):
        one, two = fields[2 * g], fields[2 * g + 1]
        even = jnp.where(low, one, pltpu.roll(two, 4, 0))
        odd = jnp.where(low, pltpu.roll(one, 124, 0), two)
        for m in range(16):
            out_ref[2 * m, 8 * g : 8 * g + 8] = even[8 * m : 8 * m + 8]
            out_ref[2 * m + 1, 8 * g : 8 * g + 8] = odd[8 * m : 8 * m + 8]


def scatter_factors(tab_ref, i, base_col, a_ref, a8_ref, z_ref, z8_ref):
    y_iota = lax.broadcasted_iota(jnp.int32, (16, VERT), 0).astype(F32)
    z_iota = lax.broadcasted_iota(jnp.int32, (256, VERT), 0).astype(F32).astype(BF16)
    zero16 = jnp.zeros((16, VERT), BF16)
    ones = jnp.ones((256, VERT), BF16)
    zeros = jnp.zeros((256, VERT), BF16)
    for s in range(SLOT_CAP):
        x = tab_ref[i, pl.ds(44 + s, 1)]
        y = tab_ref[i, pl.ds(48 + s, 1)]
        z = tab_ref[i, pl.ds(52 + s, 1)]
        upper = x >= 8.0
        x_in = jnp.where(upper, x - 8.0, x)
        column = jnp.where(upper, z + 128.0, z)
        col = slice(base_col + s * VERT, base_col + (s + 1) * VERT)
        hot = jnp.where(
            z_iota == jnp.broadcast_to(column, (256, VERT)).astype(BF16), ones, zeros
        )
        z_ref[:, col] = hot
        z8_ref[:, col] = hot.astype(F8)
        at_y = y_iota == y
        at_y1 = y_iota - 1.0 == y
        x_wide = jnp.broadcast_to(x_in, (16, VERT)).astype(BF16)
        masks = [x_wide == jnp.asarray(k, BF16) for k in range(-1, 9)]
        for pair in range(3):
            blocks = []
            for kz, c in (divmod(2 * pair, 3), divmod(2 * pair + 1, 3)):
                force = tab_ref[i, pl.ds(32 + 4 * c + s, 1)]
                parts = []
                for kx in range(2):
                    w0 = tab_ref[i, pl.ds(4 * (4 * kx + kz) + s, 1)] * force
                    w1 = tab_ref[i, pl.ds(4 * (4 * kx + 2 + kz) + s, 1)] * force
                    high, low = split(jnp.where(at_y, w0, jnp.where(at_y1, w1, 0.0)))
                    parts.append((high, (low * LOW_SCALE).astype(BF16)))
                for plane in range(9):
                    blocks.append(
                        [
                            jnp.where(
                                masks[plane + 1],
                                parts[0][hl],
                                jnp.where(masks[plane], parts[1][hl], zero16),
                            )
                            for hl in range(2)
                        ]
                    )
            for n in range(9):
                rows = slice(pair * 2 * HALF + n * 32, pair * 2 * HALF + n * 32 + 32)
                first, second = blocks[2 * n], blocks[2 * n + 1]
                a_ref[rows, col] = jnp.concatenate([first[0], second[0]], axis=0)
                a8_ref[rows, col] = jnp.concatenate([first[1], second[1]], axis=0).astype(F8)


def finish_force(acc_ref, force_ref):
    for c in range(3):
        for plane in range(16):
            pair = []
            for kz in range(2):
                base = (kz * 3 + c) * HALF
                if plane < 8:
                    total = acc_ref[base + plane * 16 : base + plane * 16 + 16, 0:128]
                elif plane == 8:
                    total = (
                        acc_ref[base + 128 : base + 144, 0:128]
                        + acc_ref[base : base + 16, 128:256]
                    )
                else:
                    start = base + (plane - 8) * 16
                    total = acc_ref[start : start + 16, 128:256]
                pair.append(total)
            force_ref[c, plane * 16 : plane * 16 + 16] = pair[0] + pltpu.roll(pair[1], 1, 1)


def collide_all(pop_ref, solid_ref, force_ref, post_ref, vel_ref):
    factor = 1.0 - 0.5 / RELAXATION

    def chunk(step, carry):
        x = step // 2
        yy = pl.ds(pl.multiple_of((step % 2) * 8, 8), 8)
        rows = pl.ds(pl.multiple_of(step * 8, 8), 8)
        pops = [pop_ref[q, x, yy] for q in range(19)]
        solid = solid_ref[x, yy] == 1
        force = [force_ref[c, rows] for c in range(3)]
        density = sum(pops[1:], pops[0])
        inverse = 1.0 / density
        velocity, largest = [], carry
        for a in range(3):
            plus = [pops[q] for q in range(19) if VELOCITIES[q][a] == 1]
            minus = [pops[q] for q in range(19) if VELOCITIES[q][a] == -1]
            momentum = sum(plus[1:], plus[0]) - sum(minus[1:], minus[0])
            u = (momentum + 0.5 * force[a]) * inverse
            velocity.append(u)
            vel_ref[a, rows] = u
            largest = jnp.maximum(largest, jnp.abs(u))
        speed_sq = velocity[0] * velocity[0] + velocity[1] * velocity[1] + velocity[2] * velocity[2]
        u_dot_f = velocity[0] * force[0] + velocity[1] * force[1] + velocity[2] * force[2]
        rate = density * (1.0 / RELAXATION)
        common = rate * (1.0 - 1.5 * speed_sq) - (3.0 * factor) * u_dot_f
        square = [4.5 * rate * velocity[a] + (9.0 * factor) * force[a] for a in range(3)]
        linear = [3.0 * rate * velocity[a] + (3.0 * factor) * force[a] for a in range(3)]
        keep = 1.0 - 1.0 / RELAXATION

        def along(direction, parts):
            total = None
            for step_a, part in zip(direction, parts):
                if step_a:
                    term = part if step_a == 1 else -part
                    total = term if total is None else total + term
            return total

        relaxed = keep * pops[0] + LATTICE_WEIGHTS[0] * common
        post_ref[0, x, yy] = jnp.where(solid, pops[0], relaxed)
        for q in range(1, 19, 2):
            w = LATTICE_WEIGHTS[q]
            even = w * (common + along(VELOCITIES[q], velocity) * along(VELOCITIES[q], square))
            odd = w * along(VELOCITIES[q], linear)
            post_ref[q, x, yy] = jnp.where(solid, pops[q + 1], keep * pops[q] + (even + odd))
            post_ref[q + 1, x, yy] = jnp.where(solid, pops[q], keep * pops[q + 1] + (even - odd))
        return largest

    return lax.fori_loop(0, 32, chunk, jnp.zeros((8, 128), F32), unroll=2)


def transpose_velocity(vel_ref, largest, vt_ref, vt8_ref):
    largest = jnp.maximum(jnp.max(jnp.max(largest, axis=0, keepdims=True), axis=1, keepdims=True), 1e-30)
    scale = TOP / largest
    for c in range(3):
        high, low = split(vel_ref[c].T)
        rows = slice(c * 128, (c + 1) * 128)
        vt_ref[rows] = high
        vt8_ref[rows, 0:256] = (high.astype(F32) * scale).astype(F8)
        vt8_ref[rows, 256:512] = (low * (scale * LOW_SCALE)).astype(F8)
    return largest * (1.0 / (TOP * LOW_SCALE))


def gather_chunk(tab_ref, i, b_ref, b8_ref, vt_ref, vt8_ref, undo, ret_ref):
    y_iota = lax.broadcasted_iota(jnp.int32, (16, VERT), 0).astype(F32)
    z_iota = lax.broadcasted_iota(jnp.int32, (VERT, VERT), 0).astype(F32)
    zero16 = jnp.zeros((16, VERT), BF16)
    for s in range(SLOT_CAP):
        x = tab_ref[i, pl.ds(44 + s, 1)]
        y = tab_ref[i, pl.ds(48 + s, 1)]
        z = tab_ref[i, pl.ds(52 + s, 1)]
        at_y = y_iota == y
        at_y1 = y_iota - 1.0 == y
        x_wide = jnp.broadcast_to(x, (16, VERT)).astype(BF16)
        masks = [x_wide == jnp.asarray(k, BF16) for k in range(-1, 16)]
        for kz in range(2):
            parts = []
            for kx in range(2):
                w0 = tab_ref[i, pl.ds(4 * (4 * kx + kz) + s, 1)]
                w1 = tab_ref[i, pl.ds(4 * (4 * kx + 2 + kz) + s, 1)]
                high, low = split(jnp.where(at_y, w0, jnp.where(at_y1, w1, 0.0)))
                parts.append((high, (low * LOW_SCALE).astype(BF16)))
            cols = slice(kz * VERT, (kz + 1) * VERT)
            for hl in range(2):
                for pair in range(8):
                    planes = [
                        jnp.where(
                            masks[plane + 1],
                            parts[0][hl],
                            jnp.where(masks[plane], parts[1][hl], zero16),
                        )
                        for plane in (2 * pair, 2 * pair + 1)
                    ]
                    both = jnp.concatenate(planes, axis=0)
                    row = pair * 32
                    if hl == 0:
                        b_ref[s, row : row + 32, cols] = both
                    row = row + 256 * (1 - hl)
                    b8_ref[s, row : row + 32, cols] = both.astype(F8)
        picked = jnp.dot(vt_ref[...], b_ref[s], preferred_element_type=F32)
        picked = picked + undo * jnp.dot(vt8_ref[...], b8_ref[s], preferred_element_type=F32)
        at_z = z_iota == z
        at_z1 = z_iota - 1.0 == z
        for c in range(3):
            rows = slice(c * 128, (c + 1) * 128)
            both = jnp.where(at_z, picked[rows, 0:128], 0.0) + jnp.where(
                at_z1, picked[rows, 128:256], 0.0
            )
            ret_ref[i, pl.ds(4 * c + s, 1)] = jnp.sum(both, axis=0, keepdims=True)


PLUS = [[q for q in range(19) if VELOCITIES[q][a] == 1] for a in range(3)]
MINUS = [[q for q in range(19) if VELOCITIES[q][a] == -1] for a in range(3)]
MESH = pl.DeviceIdType.MESH


def offset_of(i):
    j, dz = i // 4, i % 4
    half = (j + 1) // 2
    odd = j % 2
    return odd * half + (1 - odd) * ((8 - half) % 8), dz


def shift_x(post_ref, halo_ref):
    for k, q in enumerate(PLUS[0]):
        moved = post_ref[q, 0:15]
        post_ref[q, 1:16] = moved
        post_ref[q, 0] = halo_ref[0, k]
    for k, q in enumerate(MINUS[0]):
        moved = post_ref[q, 1:16]
        post_ref[q, 0:15] = moved
        post_ref[q, 15] = halo_ref[1, k]


def shift_y(post_ref, halo_ref):
    row = lax.broadcasted_iota(jnp.int32, (256, 128), 0) % 16
    for side, (directions, by, edge) in enumerate(((PLUS[1], 1, 0), (MINUS[1], 255, 15))):
        for k, q in enumerate(directions):
            moved = pltpu.roll(post_ref[q].reshape(256, 128), by, 0)
            halo = jnp.broadcast_to(halo_ref[side, k][:, None, :], (16, 16, 128)).reshape(256, 128)
            post_ref[q] = jnp.where(row == edge, halo, moved).reshape(16, 16, 128)


def turn_z(post_ref, send_ref):
    lane = lax.broadcasted_iota(jnp.int32, (256, 128), 1)
    for side, (directions, by, to) in enumerate(((PLUS[2], 1, 0), (MINUS[2], 127, 1))):
        packed = jnp.zeros((256, 128), F32)
        for k, q in enumerate(directions):
            moved = pltpu.roll(post_ref[q].reshape(256, 128), by, 1)
            post_ref[q] = moved.reshape(16, 16, 128)
            packed = jnp.where(lane == k, pltpu.roll(moved, k + to, 1) if k + to else moved, packed)
        send_ref[side] = packed


def shift_z(post_ref, halo_ref):
    lane = lax.broadcasted_iota(jnp.int32, (256, 128), 1)
    for side, (directions, edge) in enumerate(((PLUS[2], 0), (MINUS[2], 127))):
        packed = halo_ref[side]
        for k, q in enumerate(directions):
            by = (edge - k) % 128
            halo = pltpu.roll(packed, by, 1) if by else packed
            old = post_ref[q].reshape(256, 128)
            post_ref[q] = jnp.where(lane == edge, halo, old).reshape(16, 16, 128)


def step_kernel(
    inter_ref, pos_ref, anc_ref, cell_ref, w_ref, pop_hbm, solid_hbm, read_hbm, vertex_ref,
    out_ref, tab_ref, pop_ref, solid_ref, post_ref, a_ref, a8_ref, z_ref, z8_ref, acc_ref, force_ref, vel_ref, vt_ref, vt8_ref, b_ref, b8_ref,
    ret_ref, back_ref, xs_ref, xr_ref, ys_ref, yr_ref, zs_ref, zr_ref, pad_ref, place_ref, tgt_ref,
    field_ref, part_ref, tab_send, tab_recv, ret_send, ret_recv, halo_send, halo_recv, load_sem, store_sem,
):
    my_x, my_y, my_z = lax.axis_index("gx"), lax.axis_index("gy"), lax.axis_index("gz")
    load_pop = pltpu.make_async_copy(pop_hbm, pop_ref, load_sem.at[0])
    load_solid = pltpu.make_async_copy(solid_hbm, solid_ref, load_sem.at[1])
    load_target = pltpu.make_async_copy(place_ref, tgt_ref, load_sem.at[2])
    load_pop.start()
    load_solid.start()

    def ahead(i):
        dy, dz = offset_of(i)
        return (my_x, lax.rem(my_y + dy, 8), lax.rem(my_z + dz, 4))

    def behind(i):
        dy, dz = offset_of(i)
        return (my_x, lax.rem(my_y + 8 - dy, 8), lax.rem(my_z + 4 - dz, 4))

    up_x = (lax.rem(my_x + 1, 8), my_y, my_z)
    down_x = (lax.rem(my_x + 7, 8), my_y, my_z)
    up_y = (my_x, lax.rem(my_y + 1, 8), my_z)
    down_y = (my_x, lax.rem(my_y + 7, 8), my_z)
    up_z = (my_x, my_y, lax.rem(my_z + 1, 4))
    down_z = (my_x, my_y, lax.rem(my_z + 3, 4))

    barrier = pltpu.get_barrier_semaphore()

    def greet(i, carry):
        pl.semaphore_signal(barrier, inc=1, device_id=ahead(i), device_id_type=MESH)
        return carry

    lax.fori_loop(1, BRICKS, greet, 0)
    pl.semaphore_signal(barrier, inc=1, device_id=up_x, device_id_type=MESH)
    pl.semaphore_signal(barrier, inc=1, device_id=down_x, device_id_type=MESH)
    slots = choose_slots(inter_ref, pad_ref, place_ref, my_y, my_z)
    load_target.start()
    make_tables(slots, pos_ref, anc_ref, cell_ref, w_ref, field_ref, part_ref, out_ref, my_x)
    pl.semaphore_wait(barrier, BRICKS + 1)

    def table_copy(i):
        to = ahead(i)
        return pltpu.make_async_remote_copy(
            src_ref=out_ref.at[to[1] * 4 + to[2]],
            dst_ref=tab_ref.at[i],
            send_sem=tab_send.at[i],
            recv_sem=tab_recv.at[i],
            device_id=to,
            device_id_type=MESH,
        )

    def return_copy(i):
        return pltpu.make_async_remote_copy(
            src_ref=ret_ref.at[i],
            dst_ref=back_ref.at[i],
            send_sem=ret_send.at[i],
            recv_sem=ret_recv.at[i],
            device_id=behind(i),
            device_id_type=MESH,
        )

    def send_table(i, carry):
        table_copy(i).start()
        return carry

    lax.fori_loop(1, BRICKS, send_table, 0)
    tab_ref[0] = out_ref[my_y * 4 + my_z]
    acc_ref[...] = jnp.zeros_like(acc_ref)

    def scatter(t, carry):
        @pl.when(t > 0)
        def _():
            table_copy(2 * t).wait_recv()

        table_copy(2 * t + 1).wait_recv()
        for j in range(2):
            scatter_factors(tab_ref, 2 * t + j, j * 512, a_ref, a8_ref, z_ref, z8_ref)
        dims = (((1,), (1,)), ((), ()))
        high = lax.dot_general(a_ref[...], z_ref[...], dims, preferred_element_type=F32)
        low = lax.dot_general(a8_ref[...], z8_ref[...], dims, preferred_element_type=F32)
        acc_ref[...] += high + low * (1.0 / LOW_SCALE)
        return carry

    lax.fori_loop(0, BRICKS // 2, scatter, 0)
    finish_force(acc_ref, force_ref)
    load_pop.wait()
    load_solid.wait()
    largest = collide_all(pop_ref, solid_ref, force_ref, post_ref, vel_ref)

    def halo_copy(k, src, dst, to):
        return pltpu.make_async_remote_copy(
            src_ref=src,
            dst_ref=dst,
            send_sem=halo_send.at[k],
            recv_sem=halo_recv.at[k],
            device_id=to,
            device_id_type=MESH,
        )

    halo = [
        halo_copy(0, xs_ref.at[0], xr_ref.at[0], up_x),
        halo_copy(1, xs_ref.at[1], xr_ref.at[1], down_x),
        halo_copy(2, ys_ref.at[0], yr_ref.at[0], up_y),
        halo_copy(3, ys_ref.at[1], yr_ref.at[1], down_y),
        halo_copy(4, zs_ref.at[0], zr_ref.at[0], up_z),
        halo_copy(5, zs_ref.at[1], zr_ref.at[1], down_z),
    ]
    for k in range(5):
        xs_ref[0, k] = post_ref[PLUS[0][k], 15]
        xs_ref[1, k] = post_ref[MINUS[0][k], 0]
    halo[0].start()
    halo[1].start()
    undo = transpose_velocity(vel_ref, largest, vt_ref, vt8_ref)

    def store_copy(q):
        return pltpu.make_async_copy(post_ref.at[q], read_hbm.at[q], store_sem.at[q])

    along_z = PLUS[2] + MINUS[2]

    def gather(t, carry):
        for j in range(4):
            i = BRICKS - 1 - (4 * t + j)
            gather_chunk(tab_ref, i, b_ref.at[j], b8_ref.at[j], vt_ref, vt8_ref, undo, ret_ref)
        for j in range(3):
            return_copy(BRICKS - 1 - (4 * t + j)).start()

        @pl.when(t < BRICKS // 4 - 1)
        def _():
            return_copy(BRICKS - 4 - 4 * t).start()

        @pl.when(t == 1)
        def _():
            halo[0].wait_recv()
            halo[1].wait_recv()
            shift_x(post_ref, xr_ref)
            for k in range(5):
                ys_ref[0, k] = post_ref[PLUS[1][k], :, 15, :]
                ys_ref[1, k] = post_ref[MINUS[1][k], :, 0, :]
            halo[2].start()
            halo[3].start()

        @pl.when(t == 3)
        def _():
            halo[2].wait_recv()
            halo[3].wait_recv()
            shift_y(post_ref, yr_ref)
            for q in range(19):
                if q not in along_z:
                    store_copy(q).start()
            turn_z(post_ref, zs_ref)
            halo[4].start()
            halo[5].start()

        @pl.when(t == 5)
        def _():
            halo[4].wait_recv()
            halo[5].wait_recv()
            shift_z(post_ref, zr_ref)
            for q in along_z:
                store_copy(q).start()

        return carry

    lax.fori_loop(0, BRICKS // 4, gather, 0)
    back_ref[0] = ret_ref[0]

    def wait_return(i, carry):
        return_copy(i).wait_recv()
        return_copy(i).wait_send()
        table_copy(i).wait_send()
        return carry

    lax.fori_loop(1, BRICKS, wait_return, 0)

    load_target.wait()

    def patch(p, carry):
        first = jnp.clip(tgt_ref[0, p], 0, BRICKS * SLOT_CAP - 1)
        second = jnp.clip(tgt_ref[1, p], 0, BRICKS * SLOT_CAP - 1)
        for c in range(3):
            vertex_ref[c, pl.ds(p, 1)] = (
                back_ref[first // SLOT_CAP, pl.ds(4 * c + first % SLOT_CAP, 1)]
                + back_ref[second // SLOT_CAP, pl.ds(4 * c + second % SLOT_CAP, 1)]
            )
        return carry

    lax.fori_loop(0, PATCH_DEV, patch, 0, unroll=4)

    for copy in halo:
        copy.wait_send()
    for q in range(19):
        store_copy(q).wait()


def step(intersection, positions, anchors, base_cell, weights, populations, solid_flags):
    vmem = pl.BlockSpec(memory_space=pltpu.VMEM)
    hbm = pl.BlockSpec(memory_space=pltpu.HBM)
    dma = pltpu.SemaphoreType.DMA
    return pl.pallas_call(
        step_kernel,
        name="step",
        out_shape=(
            jax.ShapeDtypeStruct(populations.shape, F32),
            jax.ShapeDtypeStruct((3, PATCH_DEV, VERT), F32),
        ),
        in_specs=[vmem, vmem, vmem, vmem, vmem, hbm, hbm],
        out_specs=(hbm, vmem),
        scratch_shapes=[
            pltpu.VMEM((BRICKS, ROWS, VERT), F32),
            pltpu.VMEM((BRICKS, ROWS, VERT), F32),
            pltpu.VMEM((19, 16, 16, 128), F32),
            pltpu.VMEM((16, 16, 128), jnp.int32),
            pltpu.VMEM((19, 16, 16, 128), F32),
            pltpu.VMEM((6 * HALF, 1024), BF16),
            pltpu.VMEM((6 * HALF, 1024), F8),
            pltpu.VMEM((256, 1024), BF16),
            pltpu.VMEM((256, 1024), F8),
            pltpu.VMEM((6 * HALF, 256), F32),
            pltpu.VMEM((3, 256, 128), F32),
            pltpu.VMEM((3, 256, 128), F32),
            pltpu.VMEM((384, 256), BF16),
            pltpu.VMEM((384, 512), F8),
            pltpu.VMEM((4, 4, 256, 256), BF16),
            pltpu.VMEM((4, 4, 512, 256), F8),
            pltpu.VMEM((BRICKS, 12, VERT), F32),
            pltpu.VMEM((BRICKS, 12, VERT), F32),
            pltpu.VMEM((2, 5, 16, 128), F32),
            pltpu.VMEM((2, 5, 16, 128), F32),
            pltpu.VMEM((2, 5, 16, 128), F32),
            pltpu.VMEM((2, 5, 16, 128), F32),
            pltpu.VMEM((2, 256, 128), F32),
            pltpu.VMEM((2, 256, 128), F32),
            pltpu.VMEM((8, 128), jnp.int32),
            pltpu.VMEM((8, 128), jnp.int32),
            pltpu.SMEM((8, 128), jnp.int32),
            pltpu.VMEM((14, 32, VERT), F32),
            pltpu.VMEM((96, 14 * VERT), BF16),
            dma((BRICKS,)),
            dma((BRICKS,)),
            dma((BRICKS,)),
            dma((BRICKS,)),
            dma((6,)),
            dma((6,)),
            dma((3,)),
            dma((19,)),
        ],
        compiler_params=pltpu.CompilerParams(
            collective_id=0, has_side_effects=True, vmem_limit_bytes=60 * 1024 * 1024
        ),
    )(intersection, positions, anchors, base_cell, weights, populations, solid_flags)


def body(populations, solid_flags, positions, anchors, base_cell, weights, intersection):
    read, vertex = step(
        intersection.T,
        jnp.transpose(positions, (1, 0, 2)),
        jnp.transpose(anchors, (1, 0, 2)),
        jnp.transpose(base_cell, (1, 0, 2)),
        weights,
        populations,
        solid_flags,
    )
    return (read, jnp.transpose(vertex, (1, 0, 2)))


def solution(mesh):
    return jax.shard_map(
        body,
        mesh=mesh,
        in_specs=(
            P(None, "gx", "gy", "gz"),
            P("gx", "gy", "gz"),
            P(("gx", "gy", "gz"), None, None),
            P(("gx", "gy", "gz"), None, None),
            P(("gx", "gy", "gz"), None, None),
            P(("gx", "gy", "gz"), None, None),
            P(("gx", "gy", "gz"), None),
        ),
        out_specs=(P(None, "gx", "gy", "gz"), P(("gx", "gy", "gz"), None, None)),
        check_vma=False,
    )
```

```python
import jax
import jax.numpy as jnp
from jax import lax
from jax.experimental import pallas as pl
from jax.experimental.pallas import tpu as pltpu
from jax.sharding import PartitionSpec as P

SLOT_CAP = 4
VERT = 128
BRICKS = 32
PATCH_DEV = 28
ROWS = 56
HALF = 9 * 16

RELAXATION = 0.8
TENSION = 0.05
TETHER = 0.5
VELOCITIES = [
    (0, 0, 0),
    (1, 0, 0),
    (-1, 0, 0),
    (0, 1, 0),
    (0, -1, 0),
    (0, 0, 1),
    (0, 0, -1),
    (1, 1, 0),
    (-1, -1, 0),
    (1, -1, 0),
    (-1, 1, 0),
    (1, 0, 1),
    (-1, 0, -1),
    (1, 0, -1),
    (-1, 0, 1),
    (0, 1, 1),
    (0, -1, -1),
    (0, 1, -1),
    (0, -1, 1),
]
LATTICE_WEIGHTS = [1.0 / 3.0] + [1.0 / 18.0] * 6 + [1.0 / 36.0] * 12
F32 = jnp.float32
BF16 = jnp.bfloat16
F8 = jnp.float8_e4m3fn
LOW_SCALE = 4096.0
TOP = 24.0
OUTSIDE = -100.0


def split(value):
    high = value.astype(BF16)
    return high, value - high.astype(F32)


def thirds(value):
    high = value.astype(BF16)
    rest = value - high.astype(F32)
    middle = rest.astype(BF16)
    return high, middle, (rest - middle.astype(F32)).astype(BF16)


def choose_slots(inter_ref, pad_ref, tgt_ref, my_y, my_z):
    pad_ref[...] = jnp.full((8, 128), -1, jnp.int32)
    tgt_ref[...] = jnp.zeros((8, 128), jnp.int32)
    pad_ref[0:2, 0:PATCH_DEV] = inter_ref[...]
    lane = lax.broadcasted_iota(jnp.int32, (BRICKS, 128), 1)
    brick_iota = lax.broadcasted_iota(jnp.int32, (BRICKS, 128), 0)
    rows = [pad_ref[j : j + 1] for j in range(2)]
    listed = [(brick_iota == row).astype(jnp.int32) for row in rows]
    total = listed[0] + listed[1]
    count = total
    for by in (1, 2, 4, 8, 16):
        count = count + jnp.where(lane >= by, pltpu.roll(count, by, 1), 0)
    before = count - total
    slots = []
    for j in range(2):
        rank = jnp.sum(listed[j] * before, axis=0, keepdims=True)
        slots.append(rows[j] * SLOT_CAP + rank)
        away = ((rows[j] >> 2) - my_y + 8) & 7
        turn = jnp.where(away == 0, 0, jnp.where(away <= 4, 2 * away - 1, 16 - 2 * away))
        side = ((rows[j] & 3) - my_z + 4) & 3
        tgt_ref[j : j + 1] = (turn * 4 + side) * SLOT_CAP + rank
    return slots


def make_tables(slots, pos_ref, anc_ref, cell_ref, w_ref, field_ref, part_ref, out_ref, my_x):
    field_ref[...] = jnp.zeros_like(field_ref)
    for k in range(8):
        field_ref[k, 0:PATCH_DEV] = w_ref[:, k, :]
    for c in range(3):
        pos = pos_ref[c]
        cycle = pltpu.roll(pos, 1, 1) + pltpu.roll(pos, VERT - 1, 1) - 2.0 * pos
        field_ref[8 + c, 0:PATCH_DEV] = TENSION * cycle + TETHER * (anc_ref[c] - pos)
        field_ref[11 + c, 0:PATCH_DEV] = cell_ref[c].astype(F32) + 1.0
    for f in range(14):
        for k, part in enumerate(thirds(field_ref[f])):
            part_ref[32 * k : 32 * k + 32, f * VERT : f * VERT + VERT] = part
    slot_iota = lax.broadcasted_iota(jnp.int32, (128, 128), 0)
    routed = (slot_iota == slots[0]) | (slot_iota == slots[1])
    routed = jnp.where(routed, 1.0, 0.0).astype(BF16)[:, 0:32]
    routed = jnp.concatenate([routed, routed, routed], axis=1)
    fields = [
        jnp.dot(routed, part_ref[:, f * VERT : f * VERT + VERT], preferred_element_type=F32)
        for f in range(14)
    ]
    brick = slot_iota // SLOT_CAP
    roots = (my_x * 16, (brick // 4) * 16, (brick % 4) * 128)
    cells = [fields[11 + a] - (1 + roots[a]).astype(F32) for a in range(3)]
    inside = None
    for cell, size in zip(cells, (16.0, 16.0, 128.0)):
        within = (cell >= 0.0) & (cell < size)
        inside = within if inside is None else inside & within
    for a in range(3):
        fields[11 + a] = jnp.where(inside, cells[a], OUTSIDE)
    low = slot_iota % 8 < 4
    for g in range(7):
        one, two = fields[2 * g], fields[2 * g + 1]
        even = jnp.where(low, one, pltpu.roll(two, 4, 0))
        odd = jnp.where(low, pltpu.roll(one, 124, 0), two)
        for m in range(16):
            out_ref[2 * m, 8 * g : 8 * g + 8] = even[8 * m : 8 * m + 8]
            out_ref[2 * m + 1, 8 * g : 8 * g + 8] = odd[8 * m : 8 * m + 8]


def scatter_factors(tab_ref, i, base_col, a_ref, a8_ref, z_ref, z8_ref):
    y_iota = lax.broadcasted_iota(jnp.int32, (16, VERT), 0).astype(F32)
    z_iota = lax.broadcasted_iota(jnp.int32, (256, VERT), 0).astype(F32).astype(BF16)
    zero16 = jnp.zeros((16, VERT), BF16)
    ones = jnp.ones((256, VERT), BF16)
    zeros = jnp.zeros((256, VERT), BF16)
    for s in range(SLOT_CAP):
        x = tab_ref[i, pl.ds(44 + s, 1)]
        y = tab_ref[i, pl.ds(48 + s, 1)]
        z = tab_ref[i, pl.ds(52 + s, 1)]
        upper = x >= 8.0
        x_in = jnp.where(upper, x - 8.0, x)
        column = jnp.where(upper, z + 128.0, z)
        col = slice(base_col + s * VERT, base_col + (s + 1) * VERT)
        hot = jnp.where(
            z_iota == jnp.broadcast_to(column, (256, VERT)).astype(BF16), ones, zeros
        )
        z_ref[:, col] = hot
        z8_ref[:, col] = hot.astype(F8)
        at_y = y_iota == y
        at_y1 = y_iota - 1.0 == y
        x_wide = jnp.broadcast_to(x_in, (16, VERT)).astype(BF16)
        masks = [x_wide == jnp.asarray(k, BF16) for k in range(-1, 9)]
        for pair in range(3):
            blocks = []
            for kz, c in (divmod(2 * pair, 3), divmod(2 * pair + 1, 3)):
                force = tab_ref[i, pl.ds(32 + 4 * c + s, 1)]
                parts = []
                for kx in range(2):
                    w0 = tab_ref[i, pl.ds(4 * (4 * kx + kz) + s, 1)] * force
                    w1 = tab_ref[i, pl.ds(4 * (4 * kx + 2 + kz) + s, 1)] * force
                    high, low = split(jnp.where(at_y, w0, jnp.where(at_y1, w1, 0.0)))
                    parts.append((high, (low * LOW_SCALE).astype(BF16)))
                for plane in range(9):
                    blocks.append(
                        [
                            jnp.where(
                                masks[plane + 1],
                                parts[0][hl],
                                jnp.where(masks[plane], parts[1][hl], zero16),
                            )
                            for hl in range(2)
                        ]
                    )
            for n in range(9):
                rows = slice(pair * 2 * HALF + n * 32, pair * 2 * HALF + n * 32 + 32)
                first, second = blocks[2 * n], blocks[2 * n + 1]
                a_ref[rows, col] = jnp.concatenate([first[0], second[0]], axis=0)
                a8_ref[rows, col] = jnp.concatenate([first[1], second[1]], axis=0).astype(F8)


def finish_force(acc_ref, force_ref):
    for c in range(3):
        for plane in range(16):
            pair = []
            for kz in range(2):
                base = (kz * 3 + c) * HALF
                if plane < 8:
                    total = acc_ref[base + plane * 16 : base + plane * 16 + 16, 0:128]
                elif plane == 8:
                    total = (
                        acc_ref[base + 128 : base + 144, 0:128]
                        + acc_ref[base : base + 16, 128:256]
                    )
                else:
                    start = base + (plane - 8) * 16
                    total = acc_ref[start : start + 16, 128:256]
                pair.append(total)
            force_ref[c, plane * 16 : plane * 16 + 16] = pair[0] + pltpu.roll(pair[1], 1, 1)


def collide_all(pop_ref, solid_ref, force_ref, post_ref, vel_ref):
    factor = 1.0 - 0.5 / RELAXATION

    def chunk(step, carry):
        x = step // 2
        yy = pl.ds(pl.multiple_of((step % 2) * 8, 8), 8)
        rows = pl.ds(pl.multiple_of(step * 8, 8), 8)
        pops = [pop_ref[q, x, yy] for q in range(19)]
        solid = solid_ref[x, yy] == 1
        force = [force_ref[c, rows] for c in range(3)]
        density = sum(pops[1:], pops[0])
        inverse = 1.0 / density
        velocity, largest = [], carry
        for a in range(3):
            plus = [pops[q] for q in range(19) if VELOCITIES[q][a] == 1]
            minus = [pops[q] for q in range(19) if VELOCITIES[q][a] == -1]
            momentum = sum(plus[1:], plus[0]) - sum(minus[1:], minus[0])
            u = (momentum + 0.5 * force[a]) * inverse
            velocity.append(u)
            vel_ref[a, rows] = u
            largest = jnp.maximum(largest, jnp.abs(u))
        speed_sq = velocity[0] * velocity[0] + velocity[1] * velocity[1] + velocity[2] * velocity[2]
        u_dot_f = velocity[0] * force[0] + velocity[1] * force[1] + velocity[2] * force[2]
        rate = density * (1.0 / RELAXATION)
        common = rate * (1.0 - 1.5 * speed_sq) - (3.0 * factor) * u_dot_f
        square = [4.5 * rate * velocity[a] + (9.0 * factor) * force[a] for a in range(3)]
        linear = [3.0 * rate * velocity[a] + (3.0 * factor) * force[a] for a in range(3)]
        keep = 1.0 - 1.0 / RELAXATION

        def along(direction, parts):
            total = None
            for step_a, part in zip(direction, parts):
                if step_a:
                    term = part if step_a == 1 else -part
                    total = term if total is None else total + term
            return total

        relaxed = keep * pops[0] + LATTICE_WEIGHTS[0] * common
        post_ref[0, x, yy] = jnp.where(solid, pops[0], relaxed)
        for q in range(1, 19, 2):
            w = LATTICE_WEIGHTS[q]
            even = w * (common + along(VELOCITIES[q], velocity) * along(VELOCITIES[q], square))
            odd = w * along(VELOCITIES[q], linear)
            post_ref[q, x, yy] = jnp.where(solid, pops[q + 1], keep * pops[q] + (even + odd))
            post_ref[q + 1, x, yy] = jnp.where(solid, pops[q], keep * pops[q + 1] + (even - odd))
        return largest

    return lax.fori_loop(0, 32, chunk, jnp.zeros((8, 128), F32), unroll=2)


def transpose_velocity(vel_ref, largest, vt_ref, vt8_ref):
    largest = jnp.maximum(jnp.max(jnp.max(largest, axis=0, keepdims=True), axis=1, keepdims=True), 1e-30)
    scale = TOP / largest
    for c in range(3):
        high, low = split(vel_ref[c].T)
        rows = slice(c * 128, (c + 1) * 128)
        vt_ref[rows] = high
        vt8_ref[rows, 0:256] = (high.astype(F32) * scale).astype(F8)
        vt8_ref[rows, 256:512] = (low * (scale * LOW_SCALE)).astype(F8)
    return largest * (1.0 / (TOP * LOW_SCALE))


def gather_chunk(tab_ref, i, b_ref, b8_ref, vt_ref, vt8_ref, undo, ret_ref):
    y_iota = lax.broadcasted_iota(jnp.int32, (16, VERT), 0).astype(F32)
    z_iota = lax.broadcasted_iota(jnp.int32, (VERT, VERT), 0).astype(F32)
    zero16 = jnp.zeros((16, VERT), BF16)
    for s in range(SLOT_CAP):
        x = tab_ref[i, pl.ds(44 + s, 1)]
        y = tab_ref[i, pl.ds(48 + s, 1)]
        z = tab_ref[i, pl.ds(52 + s, 1)]
        at_y = y_iota == y
        at_y1 = y_iota - 1.0 == y
        x_wide = jnp.broadcast_to(x, (16, VERT)).astype(BF16)
        masks = [x_wide == jnp.asarray(k, BF16) for k in range(-1, 16)]
        for kz in range(2):
            parts = []
            for kx in range(2):
                w0 = tab_ref[i, pl.ds(4 * (4 * kx + kz) + s, 1)]
                w1 = tab_ref[i, pl.ds(4 * (4 * kx + 2 + kz) + s, 1)]
                high, low = split(jnp.where(at_y, w0, jnp.where(at_y1, w1, 0.0)))
                parts.append((high, (low * LOW_SCALE).astype(BF16)))
            cols = slice(kz * VERT, (kz + 1) * VERT)
            for hl in range(2):
                for pair in range(8):
                    planes = [
                        jnp.where(
                            masks[plane + 1],
                            parts[0][hl],
                            jnp.where(masks[plane], parts[1][hl], zero16),
                        )
                        for plane in (2 * pair, 2 * pair + 1)
                    ]
                    both = jnp.concatenate(planes, axis=0)
                    row = pair * 32
                    if hl == 0:
                        b_ref[s, row : row + 32, cols] = both
                    row = row + 256 * (1 - hl)
                    b8_ref[s, row : row + 32, cols] = both.astype(F8)
        picked = jnp.dot(vt_ref[...], b_ref[s], preferred_element_type=F32)
        picked = picked + undo * jnp.dot(vt8_ref[...], b8_ref[s], preferred_element_type=F32)
        at_z = z_iota == z
        at_z1 = z_iota - 1.0 == z
        for c in range(3):
            rows = slice(c * 128, (c + 1) * 128)
            both = jnp.where(at_z, picked[rows, 0:128], 0.0) + jnp.where(
                at_z1, picked[rows, 128:256], 0.0
            )
            ret_ref[i, pl.ds(4 * c + s, 1)] = jnp.sum(both, axis=0, keepdims=True)


PLUS = [[q for q in range(19) if VELOCITIES[q][a] == 1] for a in range(3)]
MINUS = [[q for q in range(19) if VELOCITIES[q][a] == -1] for a in range(3)]
MESH = pl.DeviceIdType.MESH


def offset_of(i):
    j, dz = i // 4, i % 4
    half = (j + 1) // 2
    odd = j % 2
    return odd * half + (1 - odd) * ((8 - half) % 8), dz


def shift_x(post_ref, halo_ref):
    for k, q in enumerate(PLUS[0]):
        moved = post_ref[q, 0:15]
        post_ref[q, 1:16] = moved
        post_ref[q, 0] = halo_ref[0, k]
    for k, q in enumerate(MINUS[0]):
        moved = post_ref[q, 1:16]
        post_ref[q, 0:15] = moved
        post_ref[q, 15] = halo_ref[1, k]


def shift_y(post_ref, halo_ref):
    row = lax.broadcasted_iota(jnp.int32, (256, 128), 0) % 16
    for side, (directions, by, edge) in enumerate(((PLUS[1], 1, 0), (MINUS[1], 255, 15))):
        for k, q in enumerate(directions):
            moved = pltpu.roll(post_ref[q].reshape(256, 128), by, 0)
            halo = jnp.broadcast_to(halo_ref[side, k][:, None, :], (16, 16, 128)).reshape(256, 128)
            post_ref[q] = jnp.where(row == edge, halo, moved).reshape(16, 16, 128)


def turn_z(post_ref, send_ref):
    lane = lax.broadcasted_iota(jnp.int32, (256, 128), 1)
    for side, (directions, by, to) in enumerate(((PLUS[2], 1, 0), (MINUS[2], 127, 1))):
        packed = jnp.zeros((256, 128), F32)
        for k, q in enumerate(directions):
            moved = pltpu.roll(post_ref[q].reshape(256, 128), by, 1)
            post_ref[q] = moved.reshape(16, 16, 128)
            packed = jnp.where(lane == k, pltpu.roll(moved, k + to, 1) if k + to else moved, packed)
        send_ref[side] = packed


def shift_z(post_ref, halo_ref):
    lane = lax.broadcasted_iota(jnp.int32, (256, 128), 1)
    for side, (directions, edge) in enumerate(((PLUS[2], 0), (MINUS[2], 127))):
        packed = halo_ref[side]
        for k, q in enumerate(directions):
            by = (edge - k) % 128
            halo = pltpu.roll(packed, by, 1) if by else packed
            old = post_ref[q].reshape(256, 128)
            post_ref[q] = jnp.where(lane == edge, halo, old).reshape(16, 16, 128)


def step_kernel(
    inter_ref, pos_ref, anc_ref, cell_ref, w_ref, pop_hbm, solid_hbm, read_hbm, vertex_ref,
    out_ref, tab_ref, pop_ref, solid_ref, post_ref, a_ref, a8_ref, z_ref, z8_ref, acc_ref, force_ref, vel_ref, vt_ref, vt8_ref, b_ref, b8_ref,
    ret_ref, back_ref, xs_ref, xr_ref, ys_ref, yr_ref, zs_ref, zr_ref, pad_ref, place_ref, tgt_ref,
    field_ref, part_ref, tab_send, tab_recv, ret_send, ret_recv, halo_send, halo_recv, load_sem, store_sem,
):
    my_x, my_y, my_z = lax.axis_index("gx"), lax.axis_index("gy"), lax.axis_index("gz")
    load_pop = pltpu.make_async_copy(pop_hbm, pop_ref, load_sem.at[0])
    load_solid = pltpu.make_async_copy(solid_hbm, solid_ref, load_sem.at[1])
    load_target = pltpu.make_async_copy(place_ref, tgt_ref, load_sem.at[2])
    load_pop.start()
    load_solid.start()

    def ahead(i):
        dy, dz = offset_of(i)
        return (my_x, lax.rem(my_y + dy, 8), lax.rem(my_z + dz, 4))

    def behind(i):
        dy, dz = offset_of(i)
        return (my_x, lax.rem(my_y + 8 - dy, 8), lax.rem(my_z + 4 - dz, 4))

    up_x = (lax.rem(my_x + 1, 8), my_y, my_z)
    down_x = (lax.rem(my_x + 7, 8), my_y, my_z)
    up_y = (my_x, lax.rem(my_y + 1, 8), my_z)
    down_y = (my_x, lax.rem(my_y + 7, 8), my_z)
    up_z = (my_x, my_y, lax.rem(my_z + 1, 4))
    down_z = (my_x, my_y, lax.rem(my_z + 3, 4))

    barrier = pltpu.get_barrier_semaphore()

    def greet(i, carry):
        pl.semaphore_signal(barrier, inc=1, device_id=ahead(i), device_id_type=MESH)
        return carry

    lax.fori_loop(1, BRICKS, greet, 0)
    pl.semaphore_signal(barrier, inc=1, device_id=up_x, device_id_type=MESH)
    pl.semaphore_signal(barrier, inc=1, device_id=down_x, device_id_type=MESH)
    slots = choose_slots(inter_ref, pad_ref, place_ref, my_y, my_z)
    load_target.start()
    make_tables(slots, pos_ref, anc_ref, cell_ref, w_ref, field_ref, part_ref, out_ref, my_x)
    pl.semaphore_wait(barrier, BRICKS + 1)

    def table_copy(i):
        to = ahead(i)
        return pltpu.make_async_remote_copy(
            src_ref=out_ref.at[to[1] * 4 + to[2]],
            dst_ref=tab_ref.at[i],
            send_sem=tab_send.at[i],
            recv_sem=tab_recv.at[i],
            device_id=to,
            device_id_type=MESH,
        )

    def return_copy(i):
        return pltpu.make_async_remote_copy(
            src_ref=ret_ref.at[i],
            dst_ref=back_ref.at[i],
            send_sem=ret_send.at[i],
            recv_sem=ret_recv.at[i],
            device_id=behind(i),
            device_id_type=MESH,
        )

    def send_table(i, carry):
        table_copy(i).start()
        return carry

    lax.fori_loop(1, BRICKS, send_table, 0)
    tab_ref[0] = out_ref[my_y * 4 + my_z]
    acc_ref[...] = jnp.zeros_like(acc_ref)

    def scatter(t, carry):
        @pl.when(t > 0)
        def _():
            table_copy(2 * t).wait_recv()

        table_copy(2 * t + 1).wait_recv()
        for j in range(2):
            scatter_factors(tab_ref, 2 * t + j, j * 512, a_ref, a8_ref, z_ref, z8_ref)
        dims = (((1,), (1,)), ((), ()))
        high = lax.dot_general(a_ref[...], z_ref[...], dims, preferred_element_type=F32)
        low = lax.dot_general(a8_ref[...], z8_ref[...], dims, preferred_element_type=F32)
        acc_ref[...] += high + low * (1.0 / LOW_SCALE)
        return carry

    lax.fori_loop(0, BRICKS // 2, scatter, 0)
    finish_force(acc_ref, force_ref)
    load_pop.wait()
    load_solid.wait()
    largest = collide_all(pop_ref, solid_ref, force_ref, post_ref, vel_ref)

    def halo_copy(k, src, dst, to):
        return pltpu.make_async_remote_copy(
            src_ref=src,
            dst_ref=dst,
            send_sem=halo_send.at[k],
            recv_sem=halo_recv.at[k],
            device_id=to,
            device_id_type=MESH,
        )

    halo = [
        halo_copy(0, xs_ref.at[0], xr_ref.at[0], up_x),
        halo_copy(1, xs_ref.at[1], xr_ref.at[1], down_x),
        halo_copy(2, ys_ref.at[0], yr_ref.at[0], up_y),
        halo_copy(3, ys_ref.at[1], yr_ref.at[1], down_y),
        halo_copy(4, zs_ref.at[0], zr_ref.at[0], up_z),
        halo_copy(5, zs_ref.at[1], zr_ref.at[1], down_z),
    ]
    for k in range(5):
        xs_ref[0, k] = post_ref[PLUS[0][k], 15]
        xs_ref[1, k] = post_ref[MINUS[0][k], 0]
    halo[0].start()
    halo[1].start()
    undo = transpose_velocity(vel_ref, largest, vt_ref, vt8_ref)

    def store_copy(q):
        return pltpu.make_async_copy(post_ref.at[q], read_hbm.at[q], store_sem.at[q])

    along_z = PLUS[2] + MINUS[2]

    def gather(t, carry):
        for j in range(4):
            i = BRICKS - 1 - (4 * t + j)
            gather_chunk(tab_ref, i, b_ref.at[j], b8_ref.at[j], vt_ref, vt8_ref, undo, ret_ref)
        for j in range(3):
            return_copy(BRICKS - 1 - (4 * t + j)).start()

        @pl.when(t < BRICKS // 4 - 1)
        def _():
            return_copy(BRICKS - 4 - 4 * t).start()

        @pl.when(t == 1)
        def _():
            halo[0].wait_recv()
            halo[1].wait_recv()
            shift_x(post_ref, xr_ref)
            for k in range(5):
                ys_ref[0, k] = post_ref[PLUS[1][k], :, 15, :]
                ys_ref[1, k] = post_ref[MINUS[1][k], :, 0, :]
            halo[2].start()
            halo[3].start()

        @pl.when(t == 3)
        def _():
            halo[2].wait_recv()
            halo[3].wait_recv()
            shift_y(post_ref, yr_ref)
            for q in range(19):
                if q not in along_z:
                    store_copy(q).start()
            turn_z(post_ref, zs_ref)
            halo[4].start()
            halo[5].start()

        @pl.when(t == 5)
        def _():
            halo[4].wait_recv()
            halo[5].wait_recv()
            shift_z(post_ref, zr_ref)
            for q in along_z:
                store_copy(q).start()

        return carry

    lax.fori_loop(0, BRICKS // 4, gather, 0)
    back_ref[0] = ret_ref[0]

    def wait_return(i, carry):
        return_copy(i).wait_recv()
        return_copy(i).wait_send()
        table_copy(i).wait_send()
        return carry

    lax.fori_loop(1, BRICKS, wait_return, 0)

    load_target.wait()

    def patch(p, carry):
        first = jnp.clip(tgt_ref[0, p], 0, BRICKS * SLOT_CAP - 1)
        second = jnp.clip(tgt_ref[1, p], 0, BRICKS * SLOT_CAP - 1)
        for c in range(3):
            vertex_ref[c, pl.ds(p, 1)] = (
                back_ref[first // SLOT_CAP, pl.ds(4 * c + first % SLOT_CAP, 1)]
                + back_ref[second // SLOT_CAP, pl.ds(4 * c + second % SLOT_CAP, 1)]
            )
        return carry

    lax.fori_loop(0, PATCH_DEV, patch, 0, unroll=4)

    for copy in halo:
        copy.wait_send()
    for q in range(19):
        store_copy(q).wait()


def step(intersection, positions, anchors, base_cell, weights, populations, solid_flags):
    vmem = pl.BlockSpec(memory_space=pltpu.VMEM)
    hbm = pl.BlockSpec(memory_space=pltpu.HBM)
    dma = pltpu.SemaphoreType.DMA
    return pl.pallas_call(
        step_kernel,
        name="step",
        out_shape=(
            jax.ShapeDtypeStruct(populations.shape, F32),
            jax.ShapeDtypeStruct((3, PATCH_DEV, VERT), F32),
        ),
        in_specs=[vmem, vmem, vmem, vmem, vmem, hbm, hbm],
        out_specs=(hbm, vmem),
        scratch_shapes=[
            pltpu.VMEM((BRICKS, ROWS, VERT), F32),
            pltpu.VMEM((BRICKS, ROWS, VERT), F32),
            pltpu.VMEM((19, 16, 16, 128), F32),
            pltpu.VMEM((16, 16, 128), jnp.int32),
            pltpu.VMEM((19, 16, 16, 128), F32),
            pltpu.VMEM((6 * HALF, 1024), BF16),
            pltpu.VMEM((6 * HALF, 1024), F8),
            pltpu.VMEM((256, 1024), BF16),
            pltpu.VMEM((256, 1024), F8),
            pltpu.VMEM((6 * HALF, 256), F32),
            pltpu.VMEM((3, 256, 128), F32),
            pltpu.VMEM((3, 256, 128), F32),
            pltpu.VMEM((384, 256), BF16),
            pltpu.VMEM((384, 512), F8),
            pltpu.VMEM((4, 4, 256, 256), BF16),
            pltpu.VMEM((4, 4, 512, 256), F8),
            pltpu.VMEM((BRICKS, 12, VERT), F32),
            pltpu.VMEM((BRICKS, 12, VERT), F32),
            pltpu.VMEM((2, 5, 16, 128), F32),
            pltpu.VMEM((2, 5, 16, 128), F32),
            pltpu.VMEM((2, 5, 16, 128), F32),
            pltpu.VMEM((2, 5, 16, 128), F32),
            pltpu.VMEM((2, 256, 128), F32),
            pltpu.VMEM((2, 256, 128), F32),
            pltpu.VMEM((8, 128), jnp.int32),
            pltpu.VMEM((8, 128), jnp.int32),
            pltpu.SMEM((8, 128), jnp.int32),
            pltpu.VMEM((14, 32, VERT), F32),
            pltpu.VMEM((96, 14 * VERT), BF16),
            dma((BRICKS,)),
            dma((BRICKS,)),
            dma((BRICKS,)),
            dma((BRICKS,)),
            dma((6,)),
            dma((6,)),
            dma((3,)),
            dma((19,)),
        ],
        compiler_params=pltpu.CompilerParams(
            collective_id=0, has_side_effects=True, vmem_limit_bytes=60 * 1024 * 1024
        ),
    )(intersection, positions, anchors, base_cell, weights, populations, solid_flags)


def place_kernel(read_in, vertex_in, read_out, vertex_out, held, vertex_held, in_sem, out_sem):
    arrive = [pltpu.make_async_copy(read_in.at[q], held.at[q], in_sem.at[q]) for q in range(19)]
    leave = [pltpu.make_async_copy(held.at[q], read_out.at[q], out_sem.at[q]) for q in range(19)]
    arrive.append(pltpu.make_async_copy(vertex_in, vertex_held, in_sem.at[19]))
    leave.append(pltpu.make_async_copy(vertex_held, vertex_out, out_sem.at[19]))
    for copy in arrive:
        copy.start()
    for came, goes in zip(arrive, leave):
        came.wait()
        goes.start()
    for copy in leave:
        copy.wait()


def place(read, vertex):
    hbm = pl.BlockSpec(memory_space=pltpu.HBM)
    return pl.pallas_call(
        place_kernel,
        name="place",
        out_shape=(
            jax.ShapeDtypeStruct(read.shape, F32),
            jax.ShapeDtypeStruct(vertex.shape, F32),
        ),
        in_specs=[hbm, hbm],
        out_specs=(hbm, hbm),
        scratch_shapes=[
            pltpu.VMEM(read.shape, F32),
            pltpu.VMEM(vertex.shape, F32),
            pltpu.SemaphoreType.DMA((20,)),
            pltpu.SemaphoreType.DMA((20,)),
        ],
        compiler_params=pltpu.CompilerParams(vmem_limit_bytes=60 * 1024 * 1024),
    )(read, vertex)


def body(populations, solid_flags, positions, anchors, base_cell, weights, intersection):
    read, vertex = step(
        intersection.T,
        jnp.transpose(positions, (1, 0, 2)),
        jnp.transpose(anchors, (1, 0, 2)),
        jnp.transpose(base_cell, (1, 0, 2)),
        weights,
        populations,
        solid_flags,
    )
    read, vertex = place(read, vertex)
    return (read, jnp.transpose(vertex, (1, 0, 2)))


def solution(mesh):
    return jax.shard_map(
        body,
        mesh=mesh,
        in_specs=(
            P(None, "gx", "gy", "gz"),
            P("gx", "gy", "gz"),
            P(("gx", "gy", "gz"), None, None),
            P(("gx", "gy", "gz"), None, None),
            P(("gx", "gy", "gz"), None, None),
            P(("gx", "gy", "gz"), None, None),
            P(("gx", "gy", "gz"), None),
        ),
        out_specs=(P(None, "gx", "gy", "gz"), P(("gx", "gy", "gz"), None, None)),
        check_vma=False,
    )
```
